32 devices in a mesh: ex: 8 (over z, x), ey: 4 (over y, core).
Axes of the slice: x: 2, y: 2, z: 4, core: 2. Of those that a mesh axis runs over, the one named last changes fastest.
Arguments:
- crm_state: float32 [5, 12, 32, 4096], P(None, None, None, ('ex', 'ey')), may hold values from -6 to 6
- gcm_state: float32 [5, 12, 32, 8, 4, 4], P(None, None, 'ex', 'ey'), may hold values from -6 to 6
- mass: float32 [12, 32, 8, 4, 4], P(None, 'ex', 'ey'), may hold values from 0.5 to 2
- dest: int32 [4096, 1], P(('ex', 'ey')), may hold values from 0 to 31; in each aligned block of 128 rows (0 to 127, 128 to 255, ...) at most 8 rows name the same one
- cost_class: int32 [4096], P(('ex', 'ey')), may hold values from 1 to 2
Outputs:
- cloud_slots: float32 [5, 12, 32, 8192], P(None, None, None, ('ex', 'ey'))
- gcm_out: float32 [5, 12, 32, 8, 4, 4], P(None, None, 'ex', 'ey')
The draws below stay inside these ranges and needn't reach their ends.
Inputs may be any that keep to these rules, and one draw needn't show every extreme that they name: Among the 128 columns of one device's block, at most 8 have the same dest, and some block reaches 8.
All inputs are finite; a program needn't handle non-finite values.
Results may differ from the reference program's by a relative error of at most 0.00002.
Values sent between devices are 32-bit elements; how exact they have to be, the bound alone decides.
No kernel may reach another device: no remote copies, remote signals or barrier semaphores. Data moves between devices by JAX's collectives and lax.ppermute only.
A program may use at most 128 MiB of HBM per device.

```python
import math
import jax
import jax.numpy as jnp
import numpy as np

F = 5
NZ = 12
NX = 32
NP = 4
ELX = 4
ELY = 2
EXT = 32
EYT = 8
COL_DEV = 128
COLUMNS = 4096
CAP = 8
SLOTS = 256
N_EX = 8
N_EY = 4
DEVICES = 32


def with_ends(array, key, low, largest):
    index_at = [jax.random.randint(jax.random.fold_in(key, axis), (), 0, length) for axis, length in enumerate(array.shape)]
    main_axis = array.shape.index(max(array.shape))
    beside = index_at[:main_axis] + [(index_at[main_axis] + 1) % array.shape[main_axis]] + index_at[main_axis + 1:]
    return array.at[tuple(index_at)].set(low).at[tuple(beside)].set(largest)


def steps_of(own_key, shape, pieces, low, top_value):
    def one(axis_at, shards_of):
        steps = jax.random.uniform(jax.random.fold_in(jax.random.fold_in(own_key, 6), axis_at), (shards_of,), jnp.float32, low / len(pieces), top_value / len(pieces))
        return jnp.repeat(jnp.exp(steps), shape[axis_at] // shards_of).reshape((-1,) + (1,) * (len(shape) - axis_at - 1))

    factor_of = one(*pieces[0])
    for cut in pieces[1:]:
        factor_of = factor_of * one(*cut)
    return factor_of


def routed_block(stream_key, own, number, rows, count, top, reach, slope):
    order = jax.random.permutation(stream_key, count)
    crowded, common = shares(count, rows * top, reach, slope, True), shares(count, rows * top, reach, slope, False)
    places = jnp.arange(count)

    def named(tallies, turn):
        used = int((tallies > 0).sum())
        fixed = max(1, used // 4)
        moved = fixed + (places - fixed + turn * (used - fixed)) % max(1, count - fixed)
        return jnp.zeros((count,), jnp.int32).at[order[jnp.where(places < fixed, places, moved)]].set(jnp.asarray(tallies, jnp.int32))

    tallies = jnp.where(number % 4 == 0, named(crowded, number // 4), named(common, number - number // 4 - 1))
    mixed = jax.random.permutation(jax.random.fold_in(own, 3), count)
    source_of, sink = mixed[0:count // 2 * 2:2], mixed[1:count // 2 * 2:2]
    margin = jnp.minimum(tallies[source_of] - 1, reach - tallies[sink]) // 2
    margin = jnp.where((source_of == order[0]) | (sink == order[0]) | (tallies[sink] == 0), 0, jnp.maximum(margin, 0))
    moved = jax.random.randint(jax.random.fold_in(own, 4), (count // 2,), 0, 1 << 20) % (margin + 1)
    tallies = tallies.at[source_of].add(-moved).at[sink].add(moved)
    items = jnp.searchsorted(jnp.cumsum(tallies), jnp.arange(rows * top), side="right").astype(jnp.int32)
    listing = items.reshape(top, rows).T
    listing = listing[jax.random.permutation(jax.random.fold_in(own, 1), rows)]
    turn = jax.random.randint(jax.random.fold_in(own, 2), (rows, 1), 0, top)
    return jnp.take_along_axis(listing, (jnp.arange(top)[None, :] + turn) % top, axis=1)


def shares(number_of, total, most, skew, full):
    loads = [(1 << 20) // math.isqrt(standing ** skew) + 1 for standing in range(1, number_of + 1)]
    largest = most if full else min(most, max(-(-total // number_of), total * loads[0] // sum(loads)))
    least = 1 if total - largest >= number_of - 1 else 0
    given, surplus = [largest] + [least] * (number_of - 1), total - largest - least * (number_of - 1)
    while surplus > 0:
        movable = [i for i in range(1, number_of) if given[i] < largest] or [i for i in range(1, number_of) if given[i] < most]
        whole, remaining = sum([loads[i] for i in movable]), surplus
        for i in movable:
            more = min(most - given[i], max(1, remaining * loads[i] // whole), surplus)
            given[i] = given[i] + more
            surplus = surplus - more
    return np.array(given)


def noise(rng, dims, spread, limit, cuts=(), held_as=jnp.bfloat16):
    entries = spread * jax.random.normal(rng, dims, jnp.float32)
    if cuts:
        entries = entries * steps_of(rng, dims, cuts, -0.22, 0.18)
    return jnp.clip(entries, -limit, limit).astype(held_as)


def setup_inputs(seed: int = 0) -> dict:
    keys = jax.random.split(jax.random.key(seed), 6)
    crm_state = noise(keys[0], (F, NZ, NX, COLUMNS), 1.0, 6.0, ((3, 32),), jnp.float32)
    gcm_state = noise(keys[1], (F, NZ, EXT, EYT, NP, NP), 1.0, 6.0, ((2, 8), (3, 4)), jnp.float32)
    mass = jnp.clip(jnp.exp(math.log(2.0) - 1.3862944 * jax.random.uniform(keys[2], (NZ, EXT, EYT, NP, NP), jnp.float32) ** steps_of(keys[2], (NZ, EXT, EYT, NP, NP), ((1, 8), (2, 4)), -0.2, 0.2)), 0.5, 2.0)
    dest_keys = jax.random.split(jax.random.fold_in(keys[3], 1), COLUMNS // COL_DEV)
    dest_turns = jax.random.permutation(jax.random.fold_in(keys[3], 3), COLUMNS // COL_DEV)
    dest = jax.vmap(lambda own, number: routed_block(jax.random.fold_in(keys[3], 2), own, number, COL_DEV, DEVICES, 1, CAP, 2))(dest_keys, dest_turns).reshape((COLUMNS, 1))
    cost_class = with_ends(jax.random.randint(keys[4], (COLUMNS,), 1, 3), jax.random.fold_in(keys[4], 1), 1, 2).astype(jnp.int32)
    return {"crm_state": crm_state, "gcm_state": gcm_state, "mass": mass, "dest": dest, "cost_class": cost_class}


diffusion = 0.1
advection = 0.15
buoyancy = 0.3
latent_heat = 0.5
fallout = 0.2
condense_rate = 0.4
nudging = 0.5


def neighbours(values):
    eastward = jnp.roll(values, -1, axis=1)
    westward = jnp.roll(values, 1, axis=1)
    bottom = jnp.zeros_like(values[:1])
    upward = jnp.concatenate([values[1:], bottom], axis=0)
    downward = jnp.concatenate([bottom, values[:-1]], axis=0)
    return eastward, westward, upward, downward


def substep(fields, profiles):
    column_mean = jnp.mean(fields, axis=2)
    nudged = nudging * (profiles - column_mean)
    x_wind = fields[0]
    condensed = condense_rate * jax.nn.relu(fields[3])
    changes = []
    for number in range(5):
        values = fields[number]
        eastward, westward, upward, downward = neighbours(values)
        change = diffusion * (eastward + westward + upward + downward - 4.0 * values)
        change = change - advection * 0.5 * x_wind * (eastward - westward) + nudged[number][:, None, :]
        changes.append(change)
    changes[1] = changes[1] + buoyancy * fields[2]
    changes[2] = changes[2] - buoyancy * fields[1] + latent_heat * condensed
    changes[3] = changes[3] - condensed
    changes[4] = changes[4] + condensed - fallout * fields[4]
    return fields + jnp.stack(changes)


def cloud_run(fields, profiles, substeps):
    after_one = jnp.where(substeps >= 1.0, substep(fields, profiles), fields)
    return jnp.where(substeps >= 2.0, substep(after_one, profiles), after_one)


def edge_sum(weighted):
    east_x = weighted[:, :, :, :, NP - 1, :]
    west_x = weighted[:, :, :, :, 0, :]
    weighted = weighted.at[:, :, :, :, NP - 1, :].add(jnp.roll(west_x, -1, axis=2))
    weighted = weighted.at[:, :, :, :, 0, :].add(jnp.roll(east_x, 1, axis=2))
    north_face = weighted[:, :, :, :, :, NP - 1]
    south_face = weighted[:, :, :, :, :, 0]
    weighted = weighted.at[:, :, :, :, :, NP - 1].add(jnp.roll(south_face, -1, axis=3))
    weighted = weighted.at[:, :, :, :, :, 0].add(jnp.roll(north_face, 1, axis=3))
    return weighted


def to_columns(element_grid):
    blocked = element_grid.reshape(F, NZ, N_EX, ELX, N_EY, ELY, NP, NP)
    return blocked.transpose(0, 1, 2, 4, 3, 5, 6, 7).reshape(F, NZ, COLUMNS)


def from_columns(by_column):
    blocked = by_column.reshape(F, NZ, N_EX, N_EY, ELX, ELY, NP, NP)
    return blocked.transpose(0, 1, 2, 4, 3, 5, 6, 7).reshape(F, NZ, EXT, EYT, NP, NP)


def reference(crm_state, gcm_state, mass, dest, cost_class):
    profiles = to_columns(gcm_state)
    substeps = cost_class.astype(jnp.float32)
    updated = cloud_run(crm_state, profiles, substeps)
    tendency = jnp.mean(updated - crm_state, axis=2)
    advanced = gcm_state + from_columns(tendency)
    weighted = jnp.concatenate([advanced * mass[None], mass[None]], axis=0)
    summed = edge_sum(weighted)
    gcm_out = summed[:F] / summed[F:]
    targets = dest[:, 0].astype(jnp.int32)
    onehot = (targets[:, None] == jnp.arange(DEVICES, dtype=jnp.int32)[None, :]).astype(jnp.int32)
    onehot = onehot.reshape(DEVICES, COL_DEV, DEVICES)
    earlier = (jnp.cumsum(onehot, axis=1).astype(jnp.int32) - onehot)
    ranks = jnp.sum(earlier * onehot, axis=2).astype(jnp.int32).reshape(COLUMNS)
    blocks = jnp.arange(COLUMNS, dtype=jnp.int32) // COL_DEV
    slots = (targets * SLOTS + ranks * DEVICES + blocks).astype(jnp.int32)
    cloud_slots = jnp.zeros((F, NZ, NX, DEVICES * SLOTS), jnp.float32).at[:, :, :, slots].set(updated)
    return cloud_slots, gcm_out
```

```python
import functools

import jax
import jax.numpy as jnp
from jax import lax
from jax.experimental import pallas as pl
from jax.experimental.pallas import tpu as pltpu
from jax.sharding import PartitionSpec as P

diffusion = 0.1
advection = 0.15
buoyancy = 0.3
latent_heat = 0.5
fallout = 0.2
condense_rate = 0.4
nudging = 0.5

NT = (((1,), (1,)), ((), ()))
VMEM_LIMIT = 48 * 1024 * 1024


def substep_level(values_at, profile_row, z, levels, field_count, active):
    values = [values_at(f, z) for f in range(field_count)]
    width = values[0].shape[0]
    x_wind = values[0]
    condensed = condense_rate * jnp.maximum(values[3], 0.0)
    drift = (advection * 0.5) * x_wind
    results = []
    for f in range(field_count):
        v = values[f]
        east = pltpu.roll(v, width - 1, 0)
        west = pltpu.roll(v, 1, 0)
        around = east + west
        if z + 1 < levels:
            around = around + values_at(f, z + 1)
        if z > 0:
            around = around + values_at(f, z - 1)
        mean = jnp.sum(v, axis=0, keepdims=True) * (1.0 / width)
        nudged = nudging * (profile_row(f, z) - mean)
        change = diffusion * (around - 4.0 * v) - drift * (east - west) + nudged
        if f == 1:
            change = change + buoyancy * values[2]
        elif f == 2:
            change = change - buoyancy * values[1] + latent_heat * condensed
        elif f == 3:
            change = change - condensed
        elif f == 4:
            change = change + condensed - fallout * v
        results.append(jnp.where(active, v + change, v))
    return results


def cloud_kernel(devices, capacity, crm_ref, gcm_ref, mass_ref, dest_ref, cost_ref,
                 send_ref, nodes_ref, low_ref, high_ref, first_ref, second_ref, prof_ref, tend_ref):
    field_count, levels, width, owned = crm_ref.shape
    used = field_count * levels
    total = used + levels
    nodes = gcm_ref.shape[1]
    mass = mass_ref[...]
    spare = nodes - total
    grid_fields = jnp.concatenate(
        [gcm_ref[f] for f in range(field_count)] + [mass, jnp.zeros((nodes, spare), jnp.float32)], axis=1
    )
    prof_ref[...] = grid_fields.T
    tend_ref[...] = jnp.zeros_like(tend_ref)
    cost = cost_ref[...]
    once = jnp.broadcast_to(cost >= 1, (width, owned))
    twice = jnp.broadcast_to(cost >= 2, (width, owned))

    def profile_row(f, z):
        return prof_ref[pl.ds(f * levels + z, 1), :]

    for z in range(levels):
        fresh = substep_level(lambda f, k: crm_ref[f, k], profile_row, z, levels, field_count, once)
        for f in range(field_count):
            first_ref[f, z] = fresh[f]
    for z in range(levels):
        fresh = substep_level(lambda f, k: first_ref[f, k], profile_row, z, levels, field_count, twice)
        for f in range(field_count):
            second_ref[f, z] = fresh[f]
            gained = jnp.sum(fresh[f] - crm_ref[f, z], axis=0, keepdims=True) * (1.0 / width)
            tend_ref[pl.ds(f * levels + z, 1), :] = gained

    dest_row = jnp.broadcast_to(dest_ref[...].astype(jnp.float32), (owned, owned))
    dest_col = dest_row.T
    rows = lax.broadcasted_iota(jnp.int32, (owned, owned), 0)
    cols = lax.broadcasted_iota(jnp.int32, (owned, owned), 1)
    earlier = jnp.where((dest_row == dest_col) & (rows < cols), 1, 0)
    rank = jnp.sum(earlier, axis=0, keepdims=True)
    slot = dest_ref[...] * capacity + rank
    slots = devices * capacity
    slot_rows = lax.broadcasted_iota(jnp.int32, (slots, owned), 0)
    picks = jnp.where(slot_rows == slot, 1.0, 0.0).astype(jnp.bfloat16)

    group = owned // width
    for f in range(field_count):
        for z in range(0, levels, group):
            block = second_ref[f, pl.ds(z, group)].reshape(group * width, owned)
            high = block.astype(jnp.bfloat16)
            rest = block - high.astype(jnp.float32)
            middle = rest.astype(jnp.bfloat16)
            low = (rest - middle.astype(jnp.float32)).astype(jnp.bfloat16)
            moved = lax.dot_general(picks, high, NT, preferred_element_type=jnp.float32)
            moved = moved + lax.dot_general(picks, middle, NT, preferred_element_type=jnp.float32)
            moved = moved + lax.dot_general(picks, low, NT, preferred_element_type=jnp.float32)
            at = (f * levels + z) * width
            send_ref[:, at:at + group * width] = moved

    factors = jnp.concatenate(
        [mass] * field_count + [jnp.ones((nodes, nodes - used), jnp.float32)], axis=1
    )
    weighted = (grid_fields + tend_ref[...].T) * factors
    nodes_ref[...] = weighted


def edges_x(elx, ely, side, nodes_ref, low_ref, high_ref):
    step = side * side
    for b in range(ely):
        low_ref[b * side:(b + 1) * side, :] = nodes_ref[b * step:b * step + side, :]
        start = (elx - 1) * ely * step + b * step + (side - 1) * side
        high_ref[b * side:(b + 1) * side, :] = nodes_ref[start:start + side, :]


def kernel_a(devices, capacity, elx, ely, side, *refs):
    cloud_kernel(devices, capacity, *refs)
    edges_x(elx, ely, side, *refs[6:9])


def kernel_x(elx, ely, side, nodes_ref, west_ref, east_ref, sum_ref, low_ref, high_ref):
    step = side * side
    sum_ref[...] = nodes_ref[...]
    for a in range(elx):
        for b in range(ely):
            base = (a * ely + b) * step
            last = base + (side - 1) * side
            if a > 0:
                before = ((a - 1) * ely + b) * step + (side - 1) * side
                gain = nodes_ref[before:before + side, :]
            else:
                gain = west_ref[b * side:(b + 1) * side, :]
            sum_ref[base:base + side, :] = nodes_ref[base:base + side, :] + gain
            if a + 1 < elx:
                after = ((a + 1) * ely + b) * step
                gain = nodes_ref[after:after + side, :]
            else:
                gain = east_ref[b * side:(b + 1) * side, :]
            sum_ref[last:last + side, :] = nodes_ref[last:last + side, :] + gain
    for a in range(elx):
        first = a * ely * step
        final = (a * ely + ely - 1) * step + side - 1
        low_ref[a * side:(a + 1) * side, :] = sum_ref[pl.ds(first, side, stride=side), :]
        high_ref[a * side:(a + 1) * side, :] = sum_ref[pl.ds(final, side, stride=side), :]


def kernel_y(elx, ely, side, sum_ref, south_ref, north_ref, out_ref, full_ref):
    step = side * side
    field_count, nodes, levels = out_ref.shape
    full_ref[...] = sum_ref[...]
    for a in range(elx):
        for b in range(ely):
            base = (a * ely + b) * step
            if b > 0:
                gain = sum_ref[pl.ds(base - step + side - 1, side, stride=side), :]
            else:
                gain = south_ref[a * side:(a + 1) * side, :]
            here = pl.ds(base, side, stride=side)
            full_ref[here, :] = sum_ref[here, :] + gain
            if b + 1 < ely:
                gain = sum_ref[pl.ds(base + step, side, stride=side), :]
            else:
                gain = north_ref[a * side:(a + 1) * side, :]
            here = pl.ds(base + side - 1, side, stride=side)
            full_ref[here, :] = sum_ref[here, :] + gain
    full = full_ref[...]
    divisor = full[:, field_count * levels:(field_count + 1) * levels]
    for f in range(field_count):
        out_ref[f] = full[:, f * levels:(f + 1) * levels] / divisor


def kernel_out(devices, capacity, recv_ref, out_ref):
    ranked = [recv_ref[pl.ds(r, devices, stride=capacity), :] for r in range(capacity)]
    out_ref[...] = jnp.concatenate(ranked, axis=0).T


def params(**more):
    return pltpu.CompilerParams(vmem_limit_bytes=VMEM_LIMIT, **more)


def cost(flops, byte_count):
    return pl.CostEstimate(flops=flops, bytes_accessed=byte_count, transcendentals=0)


def shift(face, axis, by):
    count = lax.axis_size(axis)
    return lax.ppermute(face, axis, [(i, (i + by) % count) for i in range(count)])


def body(crm_state, gcm_state, mass, dest, cost_class):
    devices = lax.axis_size(("ex", "ey"))
    field_count, levels, width, owned = crm_state.shape
    elx, ely, side = gcm_state.shape[2:5]
    capacity = max(2, 2 * owned // devices)
    slots = capacity * devices
    values = field_count * levels * width
    f32 = jnp.float32
    gcm_nodes = gcm_state.transpose(0, 2, 3, 4, 5, 1).reshape(field_count, owned, levels)
    mass_nodes = mass.transpose(1, 2, 3, 4, 0).reshape(owned, levels)
    sizes = (elx, ely, side)
    face_x = jax.ShapeDtypeStruct((ely * side, owned), f32)
    face_y = jax.ShapeDtypeStruct((elx * side, owned), f32)
    square = jax.ShapeDtypeStruct((owned, owned), f32)
    send, nodes, low, high = pl.pallas_call(
        functools.partial(kernel_a, devices, capacity, *sizes),
        out_shape=(jax.ShapeDtypeStruct((slots, values), f32), square, face_x, face_x),
        scratch_shapes=[
            pltpu.VMEM(crm_state.shape, f32),
            pltpu.VMEM(crm_state.shape, f32),
            pltpu.VMEM((owned, owned), f32),
            pltpu.VMEM((owned, owned), f32),
        ],
        compiler_params=params(),
        name="cloud_models",
    )(crm_state, gcm_nodes, mass_nodes, dest.reshape(1, owned), cost_class.reshape(1, owned))
    received = lax.all_to_all(
        send.reshape(devices, capacity, values), ("ex", "ey"), split_axis=0, concat_axis=0, tiled=True
    )
    east = shift(low, "ex", -1)
    west = shift(high, "ex", 1)
    summed, low, high = pl.pallas_call(
        functools.partial(kernel_x, *sizes),
        out_shape=(square, face_y, face_y),
        compiler_params=params(),
        cost_estimate=cost(10**5, 10**5),
        name="edge_sum_first",
    )(nodes, west, east)
    north = shift(low, "ey", -1)
    south = shift(high, "ey", 1)
    gcm_out = pl.pallas_call(
        functools.partial(kernel_y, *sizes),
        out_shape=jax.ShapeDtypeStruct((field_count, owned, levels), f32),
        scratch_shapes=[pltpu.VMEM((owned, owned), f32)],
        compiler_params=params(),
        cost_estimate=cost(10**5, 10**5),
        name="edge_sum_second",
    )(summed, south, north)
    gcm_out = gcm_out.reshape(field_count, elx, ely, side, side, levels).transpose(0, 5, 1, 2, 3, 4)
    block = owned
    cloud = pl.pallas_call(
        functools.partial(kernel_out, devices, capacity),
        grid=(values // block,),
        in_specs=[pl.BlockSpec((slots, block), lambda i: (0, i))],
        out_specs=pl.BlockSpec((block, slots), lambda i: (i, 0)),
        out_shape=jax.ShapeDtypeStruct((values, slots), f32),
        compiler_params=params(),
        name="cloud_slots",
    )(received.reshape(slots, values))
    return cloud.reshape(field_count, levels, width, slots), gcm_out


def solution(mesh):
    return jax.shard_map(
        body,
        mesh=mesh,
        in_specs=(
            P(None, None, None, ("ex", "ey")),
            P(None, None, "ex", "ey", None, None),
            P(None, "ex", "ey", None, None),
            P(("ex", "ey"), None),
            P(("ex", "ey")),
        ),
        out_specs=(P(None, None, None, ("ex", "ey")), P(None, None, "ex", "ey", None, None)),
        check_vma=False,
    )
```

```python
import functools

import jax
import jax.numpy as jnp
from jax import lax
from jax.experimental import pallas as pl
from jax.experimental.pallas import tpu as pltpu
from jax.sharding import PartitionSpec as P

diffusion = 0.1
advection = 0.15
buoyancy = 0.3
latent_heat = 0.5
fallout = 0.2
condense_rate = 0.4
nudging = 0.5

NT = (((1,), (1,)), ((), ()))
VMEM_LIMIT = 48 * 1024 * 1024


def substep_level(values_at, profile_row, z, levels, field_count, active):
    values = [values_at(f, z) for f in range(field_count)]
    width = values[0].shape[0]
    x_wind = values[0]
    condensed = condense_rate * jnp.maximum(values[3], 0.0)
    drift = (advection * 0.5) * x_wind
    results = []
    for f in range(field_count):
        v = values[f]
        east = pltpu.roll(v, width - 1, 0)
        west = pltpu.roll(v, 1, 0)
        around = east + west
        if z + 1 < levels:
            around = around + values_at(f, z + 1)
        if z > 0:
            around = around + values_at(f, z - 1)
        mean = jnp.sum(v, axis=0, keepdims=True) * (1.0 / width)
        nudged = nudging * (profile_row(f, z) - mean)
        change = diffusion * (around - 4.0 * v) - drift * (east - west) + nudged
        if f == 1:
            change = change + buoyancy * values[2]
        elif f == 2:
            change = change - buoyancy * values[1] + latent_heat * condensed
        elif f == 3:
            change = change - condensed
        elif f == 4:
            change = change + condensed - fallout * v
        results.append(jnp.where(active, v + change, v))
    return results


def fetch(source, target, sem):
    copy = pltpu.make_async_copy(source, target, sem)
    copy.start()
    return copy


def cloud_kernel(devices, capacity, crm_hbm, gcm_hbm, mass_hbm, dest_hbm, cost_hbm,
                 send_hbm, nodes_ref, low_ref, high_ref, first_ref, second_ref, prof_ref, tend_ref,
                 crm_ref, gcm_ref, mass_ref, dest_ref, cost_ref, send_ref, small_sem, crm_sem, send_sem):
    field_count, levels, width, owned = crm_ref.shape
    small = [
        fetch(gcm_hbm, gcm_ref, small_sem.at[0]),
        fetch(mass_hbm, mass_ref, small_sem.at[1]),
        fetch(dest_hbm, dest_ref, small_sem.at[2]),
        fetch(cost_hbm, cost_ref, small_sem.at[3]),
    ]
    group = owned // width
    pieces = [
        fetch(crm_hbm.at[:, pl.ds(z, group)], crm_ref.at[:, pl.ds(z, group)], crm_sem.at[z // group])
        for z in range(0, levels, group)
    ]
    for copy in small:
        copy.wait()
    used = field_count * levels
    total = used + levels
    nodes = gcm_ref.shape[1]
    mass = mass_ref[...]
    spare = nodes - total
    grid_fields = jnp.concatenate(
        [gcm_ref[f] for f in range(field_count)] + [mass, jnp.zeros((nodes, spare), jnp.float32)], axis=1
    )
    prof_ref[...] = grid_fields.T
    tend_ref[...] = jnp.zeros_like(tend_ref)
    cost = cost_ref[...]
    once = jnp.broadcast_to(cost >= 1, (width, owned))
    twice = jnp.broadcast_to(cost >= 2, (width, owned))

    def profile_row(f, z):
        return prof_ref[pl.ds(f * levels + z, 1), :]

    for z in range(levels):
        if z == 0:
            pieces[0].wait()
        if (z + 1) % group == 0 and z + 1 < levels:
            pieces[(z + 1) // group].wait()
        fresh = substep_level(lambda f, k: crm_ref[f, k], profile_row, z, levels, field_count, once)
        for f in range(field_count):
            first_ref[f, z] = fresh[f]
    for z in range(levels):
        fresh = substep_level(lambda f, k: first_ref[f, k], profile_row, z, levels, field_count, twice)
        for f in range(field_count):
            second_ref[f, z] = fresh[f]
            gained = jnp.sum(fresh[f] - crm_ref[f, z], axis=0, keepdims=True) * (1.0 / width)
            tend_ref[pl.ds(f * levels + z, 1), :] = gained

    dest_row = jnp.broadcast_to(dest_ref[...].astype(jnp.float32), (owned, owned))
    dest_col = dest_row.T
    rows = lax.broadcasted_iota(jnp.int32, (owned, owned), 0)
    cols = lax.broadcasted_iota(jnp.int32, (owned, owned), 1)
    earlier = jnp.where((dest_row == dest_col) & (rows < cols), 1, 0)
    rank = jnp.sum(earlier, axis=0, keepdims=True)
    slot = dest_ref[...] * capacity + rank
    slots = devices * capacity
    slot_rows = lax.broadcasted_iota(jnp.int32, (slots, owned), 0)
    picks = jnp.where(slot_rows == slot, 1.0, 0.0).astype(jnp.bfloat16)

    field_rows = levels // group * capacity
    aligned = field_rows % 8 == 0
    sends = []
    for f in range(field_count):
        for z in range(0, levels, group):
            block = second_ref[f, pl.ds(z, group)].reshape(group * width, owned)
            high = block.astype(jnp.bfloat16)
            rest = block - high.astype(jnp.float32)
            middle = rest.astype(jnp.bfloat16)
            low = (rest - middle.astype(jnp.float32)).astype(jnp.bfloat16)
            moved = lax.dot_general(picks, high, NT, preferred_element_type=jnp.float32)
            moved = moved + lax.dot_general(picks, middle, NT, preferred_element_type=jnp.float32)
            moved = moved + lax.dot_general(picks, low, NT, preferred_element_type=jnp.float32)
            at = (f * levels + z) // group * capacity
            send_ref[:, at:at + capacity, :] = moved.reshape(devices, capacity, group * width)
        if aligned:
            part = pl.ds(f * field_rows, field_rows)
            sends.append(fetch(send_ref.at[:, part], send_hbm.at[:, part], send_sem.at[f]))
    if not aligned:
        sends.append(fetch(send_ref, send_hbm, send_sem.at[0]))

    factors = jnp.concatenate(
        [mass] * field_count + [jnp.ones((nodes, nodes - used), jnp.float32)], axis=1
    )
    weighted = (grid_fields + tend_ref[...].T) * factors
    nodes_ref[...] = weighted
    return sends


def edges_x(elx, ely, side, nodes_ref, low_ref, high_ref):
    step = side * side
    for b in range(ely):
        low_ref[b * side:(b + 1) * side, :] = nodes_ref[b * step:b * step + side, :]
        start = (elx - 1) * ely * step + b * step + (side - 1) * side
        high_ref[b * side:(b + 1) * side, :] = nodes_ref[start:start + side, :]


def kernel_a(devices, capacity, elx, ely, side, *refs):
    sends = cloud_kernel(devices, capacity, *refs)
    edges_x(elx, ely, side, *refs[6:9])
    for copy in sends:
        copy.wait()


def kernel_x(elx, ely, side, nodes_ref, west_ref, east_ref, sum_ref, low_ref, high_ref):
    step = side * side
    sum_ref[...] = nodes_ref[...]
    for a in range(elx):
        for b in range(ely):
            base = (a * ely + b) * step
            last = base + (side - 1) * side
            if a > 0:
                before = ((a - 1) * ely + b) * step + (side - 1) * side
                gain = nodes_ref[before:before + side, :]
            else:
                gain = west_ref[b * side:(b + 1) * side, :]
            sum_ref[base:base + side, :] = nodes_ref[base:base + side, :] + gain
            if a + 1 < elx:
                after = ((a + 1) * ely + b) * step
                gain = nodes_ref[after:after + side, :]
            else:
                gain = east_ref[b * side:(b + 1) * side, :]
            sum_ref[last:last + side, :] = nodes_ref[last:last + side, :] + gain
    for a in range(elx):
        first = a * ely * step
        final = (a * ely + ely - 1) * step + side - 1
        low_ref[a * side:(a + 1) * side, :] = sum_ref[pl.ds(first, side, stride=side), :]
        high_ref[a * side:(a + 1) * side, :] = sum_ref[pl.ds(final, side, stride=side), :]


def kernel_y(elx, ely, side, sum_ref, south_ref, north_ref, out_ref, full_ref):
    step = side * side
    field_count, nodes, levels = out_ref.shape
    full_ref[...] = sum_ref[...]
    for a in range(elx):
        for b in range(ely):
            base = (a * ely + b) * step
            if b > 0:
                gain = sum_ref[pl.ds(base - step + side - 1, side, stride=side), :]
            else:
                gain = south_ref[a * side:(a + 1) * side, :]
            here = pl.ds(base, side, stride=side)
            full_ref[here, :] = sum_ref[here, :] + gain
            if b + 1 < ely:
                gain = sum_ref[pl.ds(base + step, side, stride=side), :]
            else:
                gain = north_ref[a * side:(a + 1) * side, :]
            here = pl.ds(base + side - 1, side, stride=side)
            full_ref[here, :] = sum_ref[here, :] + gain
    full = full_ref[...]
    divisor = full[:, field_count * levels:(field_count + 1) * levels]
    for f in range(field_count):
        out_ref[f] = full[:, f * levels:(f + 1) * levels] / divisor


def kernel_out(devices, capacity, recv_ref, out_hbm, out_ref, sem):
    values = out_ref.shape[0]
    block = values // sem.shape[0]
    pitch = recv_ref.shape[0] // devices
    copies = []
    for step, at in enumerate(range(0, values, block)):
        first = step * capacity
        ranked = [recv_ref[pl.ds(first + r, devices, stride=pitch), :] for r in range(capacity)]
        out_ref[at:at + block, :] = jnp.concatenate(ranked, axis=0).T
        part = pl.ds(at, block)
        copies.append(fetch(out_ref.at[part], out_hbm.at[part], sem.at[step]))
    for copy in copies:
        copy.wait()


def params(**more):
    return pltpu.CompilerParams(vmem_limit_bytes=VMEM_LIMIT, **more)


def cost(flops, byte_count):
    return pl.CostEstimate(flops=flops, bytes_accessed=byte_count, transcendentals=0)


def shift(face, axis, by):
    count = lax.axis_size(axis)
    return lax.ppermute(face, axis, [(i, (i + by) % count) for i in range(count)])


def body(crm_state, gcm_state, mass, dest, cost_class):
    devices = lax.axis_size(("ex", "ey"))
    field_count, levels, width, owned = crm_state.shape
    elx, ely, side = gcm_state.shape[2:5]
    capacity = max(2, 2 * owned // devices)
    slots = capacity * devices
    values = field_count * levels * width
    f32 = jnp.float32
    gcm_nodes = gcm_state.transpose(0, 2, 3, 4, 5, 1).reshape(field_count, owned, levels)
    mass_nodes = mass.transpose(1, 2, 3, 4, 0).reshape(owned, levels)
    packed = (devices, values // owned * capacity, owned)
    sizes = (elx, ely, side)
    face_x = jax.ShapeDtypeStruct((ely * side, owned), f32)
    face_y = jax.ShapeDtypeStruct((elx * side, owned), f32)
    in_hbm = pl.BlockSpec(memory_space=pltpu.HBM)
    in_vmem = pl.BlockSpec(memory_space=pltpu.VMEM)
    square = jax.ShapeDtypeStruct((owned, owned), f32)
    send, nodes, low, high = pl.pallas_call(
        functools.partial(kernel_a, devices, capacity, *sizes),
        out_shape=(jax.ShapeDtypeStruct(packed, f32), square, face_x, face_x),
        in_specs=[in_hbm] * 5,
        out_specs=(in_hbm, in_vmem, in_vmem, in_vmem),
        scratch_shapes=[
            pltpu.VMEM(crm_state.shape, f32),
            pltpu.VMEM(crm_state.shape, f32),
            pltpu.VMEM((owned, owned), f32),
            pltpu.VMEM((owned, owned), f32),
            pltpu.VMEM(crm_state.shape, f32),
            pltpu.VMEM(gcm_nodes.shape, f32),
            pltpu.VMEM(mass_nodes.shape, f32),
            pltpu.VMEM((1, owned), jnp.int32),
            pltpu.VMEM((1, owned), jnp.int32),
            pltpu.VMEM(packed, f32),
            pltpu.SemaphoreType.DMA((4,)),
            pltpu.SemaphoreType.DMA((levels * width // owned,)),
            pltpu.SemaphoreType.DMA((field_count,)),
        ],
        compiler_params=params(),
        name="cloud_models",
    )(crm_state, gcm_nodes, mass_nodes, dest.reshape(1, owned), cost_class.reshape(1, owned))
    received = lax.all_to_all(
        send, ("ex", "ey"), split_axis=0, concat_axis=0, tiled=True
    )
    east = shift(low, "ex", -1)
    west = shift(high, "ex", 1)
    summed, low, high = pl.pallas_call(
        functools.partial(kernel_x, *sizes),
        out_shape=(square, face_y, face_y),
        compiler_params=params(),
        cost_estimate=cost(10**5, 10**5),
        name="edge_sum_first",
    )(nodes, west, east)
    north = shift(low, "ey", -1)
    south = shift(high, "ey", 1)
    gcm_out = pl.pallas_call(
        functools.partial(kernel_y, *sizes),
        out_shape=jax.ShapeDtypeStruct((field_count, owned, levels), f32),
        scratch_shapes=[pltpu.VMEM((owned, owned), f32)],
        compiler_params=params(),
        cost_estimate=cost(10**5, 10**5),
        name="edge_sum_second",
    )(summed, south, north)
    gcm_out = gcm_out.reshape(field_count, elx, ely, side, side, levels).transpose(0, 5, 1, 2, 3, 4)
    cloud = pl.pallas_call(
        functools.partial(kernel_out, devices, capacity),
        in_specs=[in_vmem],
        out_specs=in_hbm,
        out_shape=jax.ShapeDtypeStruct((values, slots), f32),
        scratch_shapes=[pltpu.VMEM((values, slots), f32), pltpu.SemaphoreType.DMA((values // owned,))],
        compiler_params=params(),
        name="cloud_slots",
    )(received.reshape(-1, owned))
    return cloud.reshape(field_count, levels, width, slots), gcm_out


def solution(mesh):
    return jax.shard_map(
        body,
        mesh=mesh,
        in_specs=(
            P(None, None, None, ("ex", "ey")),
            P(None, None, "ex", "ey", None, None),
            P(None, "ex", "ey", None, None),
            P(("ex", "ey"), None),
            P(("ex", "ey")),
        ),
        out_specs=(P(None, None, None, ("ex", "ey")), P(None, None, "ex", "ey", None, None)),
        check_vma=False,
    )
```

```python
import functools

import jax
import jax.numpy as jnp
from jax import lax
from jax.experimental import pallas as pl
from jax.experimental.pallas import tpu as pltpu
from jax.sharding import PartitionSpec as P

diffusion = 0.1
advection = 0.15
buoyancy = 0.3
latent_heat = 0.5
fallout = 0.2
condense_rate = 0.4
nudging = 0.5

NT = (((1,), (1,)), ((), ()))
MIB = 1024 * 1024


def substep_level(values_at, profile_row, z, levels, field_count, active):
    values = [values_at(f, z) for f in range(field_count)]
    width = values[0].shape[0]
    x_wind = values[0]
    condensed = condense_rate * jnp.maximum(values[3], 0.0)
    drift = (advection * 0.5) * x_wind
    results = []
    for f in range(field_count):
        v = values[f]
        east = pltpu.roll(v, width - 1, 0)
        west = pltpu.roll(v, 1, 0)
        around = east + west
        if z + 1 < levels:
            around = around + values_at(f, z + 1)
        if z > 0:
            around = around + values_at(f, z - 1)
        mean = jnp.sum(v, axis=0, keepdims=True) * (1.0 / width)
        nudged = nudging * (profile_row(f, z) - mean)
        change = diffusion * (around - 4.0 * v) - drift * (east - west) + nudged
        if f == 1:
            change = change + buoyancy * values[2]
        elif f == 2:
            change = change - buoyancy * values[1] + latent_heat * condensed
        elif f == 3:
            change = change - condensed
        elif f == 4:
            change = change + condensed - fallout * v
        results.append(jnp.where(active, v + change, v))
    return results


def fetch(source, target, sem):
    copy = pltpu.make_async_copy(source, target, sem)
    copy.start()
    return copy


def cloud_kernel(devices, capacity, crm_hbm, gcm_hbm, mass_hbm, dest_hbm, cost_hbm,
                 send_hbm, nodes_ref, low_ref, high_ref, first_ref, second_ref, prof_ref, tend_ref,
                 crm_ref, gcm_ref, mass_ref, dest_ref, cost_ref, send_ref, small_sem, crm_sem, send_sem):
    field_count, levels, width, owned = crm_ref.shape
    small = [
        fetch(gcm_hbm, gcm_ref, small_sem.at[0]),
        fetch(mass_hbm, mass_ref, small_sem.at[1]),
        fetch(dest_hbm, dest_ref, small_sem.at[2]),
        fetch(cost_hbm, cost_ref, small_sem.at[3]),
    ]
    group = owned // width
    pieces = [
        fetch(crm_hbm.at[:, pl.ds(z, group)], crm_ref.at[:, pl.ds(z, group)], crm_sem.at[z // group])
        for z in range(0, levels, group)
    ]
    for copy in small:
        copy.wait()
    used = field_count * levels
    total = used + levels
    nodes = gcm_ref.shape[1]
    mass = mass_ref[...]
    spare = nodes - total
    grid_fields = jnp.concatenate(
        [gcm_ref[f] for f in range(field_count)] + [mass, jnp.zeros((nodes, spare), jnp.float32)], axis=1
    )
    prof_ref[...] = grid_fields.T
    tend_ref[...] = jnp.zeros_like(tend_ref)
    cost = cost_ref[...]
    once = jnp.broadcast_to(cost >= 1, (width, owned))
    twice = jnp.broadcast_to(cost >= 2, (width, owned))

    def profile_row(f, z):
        return prof_ref[pl.ds(f * levels + z, 1), :]

    for z in range(levels):
        if z == 0:
            pieces[0].wait()
        if (z + 1) % group == 0 and z + 1 < levels:
            pieces[(z + 1) // group].wait()
        fresh = substep_level(lambda f, k: crm_ref[f, k], profile_row, z, levels, field_count, once)
        for f in range(field_count):
            first_ref[f, z] = fresh[f]
    for z in range(levels):
        fresh = substep_level(lambda f, k: first_ref[f, k], profile_row, z, levels, field_count, twice)
        for f in range(field_count):
            second_ref[f, z] = fresh[f]
            gained = jnp.sum(fresh[f] - crm_ref[f, z], axis=0, keepdims=True) * (1.0 / width)
            tend_ref[pl.ds(f * levels + z, 1), :] = gained

    dest_row = jnp.broadcast_to(dest_ref[...].astype(jnp.float32), (owned, owned))
    dest_col = dest_row.T
    rows = lax.broadcasted_iota(jnp.int32, (owned, owned), 0)
    cols = lax.broadcasted_iota(jnp.int32, (owned, owned), 1)
    earlier = jnp.where((dest_row == dest_col) & (rows < cols), 1, 0)
    rank = jnp.sum(earlier, axis=0, keepdims=True)
    slot = dest_ref[...] * capacity + rank
    slots = devices * capacity
    slot_rows = lax.broadcasted_iota(jnp.int32, (slots, owned), 0)
    picks = jnp.where(slot_rows == slot, 1.0, 0.0).astype(jnp.bfloat16)

    field_rows = levels // group * capacity
    aligned = field_rows % 8 == 0
    sends = []
    for f in range(field_count):
        for z in range(0, levels, group):
            block = second_ref[f, pl.ds(z, group)].reshape(group * width, owned)
            high = block.astype(jnp.bfloat16)
            rest = block - high.astype(jnp.float32)
            middle = rest.astype(jnp.bfloat16)
            low = (rest - middle.astype(jnp.float32)).astype(jnp.bfloat16)
            moved = lax.dot_general(picks, high, NT, preferred_element_type=jnp.float32)
            moved = moved + lax.dot_general(picks, middle, NT, preferred_element_type=jnp.float32)
            moved = moved + lax.dot_general(picks, low, NT, preferred_element_type=jnp.float32)
            at = (f * levels + z) // group * capacity
            send_ref[:, at:at + capacity, :] = moved.reshape(devices, capacity, group * width)
        if aligned:
            part = pl.ds(f * field_rows, field_rows)
            sends.append(fetch(send_ref.at[:, part], send_hbm.at[:, part], send_sem.at[f]))
    if not aligned:
        sends.append(fetch(send_ref, send_hbm, send_sem.at[0]))

    factors = jnp.concatenate(
        [mass] * field_count + [jnp.ones((nodes, nodes - used), jnp.float32)], axis=1
    )
    weighted = (grid_fields + tend_ref[...].T) * factors
    nodes_ref[...] = weighted
    return sends


def edges_x(elx, ely, side, nodes_ref, low_ref, high_ref):
    step = side * side
    for b in range(ely):
        low_ref[b * side:(b + 1) * side, :] = nodes_ref[b * step:b * step + side, :]
        start = (elx - 1) * ely * step + b * step + (side - 1) * side
        high_ref[b * side:(b + 1) * side, :] = nodes_ref[start:start + side, :]


def kernel_a(devices, capacity, elx, ely, side, *refs):
    sends = cloud_kernel(devices, capacity, *refs)
    edges_x(elx, ely, side, *refs[6:9])
    for copy in sends:
        copy.wait()


def kernel_x(elx, ely, side, nodes_ref, west_ref, east_ref, sum_ref, low_ref, high_ref):
    step = side * side
    sum_ref[...] = nodes_ref[...]
    for a in range(elx):
        for b in range(ely):
            base = (a * ely + b) * step
            last = base + (side - 1) * side
            if a > 0:
                before = ((a - 1) * ely + b) * step + (side - 1) * side
                gain = nodes_ref[before:before + side, :]
            else:
                gain = west_ref[b * side:(b + 1) * side, :]
            sum_ref[base:base + side, :] = nodes_ref[base:base + side, :] + gain
            if a + 1 < elx:
                after = ((a + 1) * ely + b) * step
                gain = nodes_ref[after:after + side, :]
            else:
                gain = east_ref[b * side:(b + 1) * side, :]
            sum_ref[last:last + side, :] = nodes_ref[last:last + side, :] + gain
    for a in range(elx):
        first = a * ely * step
        final = (a * ely + ely - 1) * step + side - 1
        low_ref[a * side:(a + 1) * side, :] = sum_ref[pl.ds(first, side, stride=side), :]
        high_ref[a * side:(a + 1) * side, :] = sum_ref[pl.ds(final, side, stride=side), :]


def kernel_y(elx, ely, side, sum_ref, south_ref, north_ref, out_ref, full_ref):
    step = side * side
    field_count, nodes, levels = out_ref.shape
    full_ref[...] = sum_ref[...]
    for a in range(elx):
        for b in range(ely):
            base = (a * ely + b) * step
            if b > 0:
                gain = sum_ref[pl.ds(base - step + side - 1, side, stride=side), :]
            else:
                gain = south_ref[a * side:(a + 1) * side, :]
            here = pl.ds(base, side, stride=side)
            full_ref[here, :] = sum_ref[here, :] + gain
            if b + 1 < ely:
                gain = sum_ref[pl.ds(base + step, side, stride=side), :]
            else:
                gain = north_ref[a * side:(a + 1) * side, :]
            here = pl.ds(base + side - 1, side, stride=side)
            full_ref[here, :] = sum_ref[here, :] + gain
    full = full_ref[...]
    divisor = full[:, field_count * levels:(field_count + 1) * levels]
    for f in range(field_count):
        out_ref[f] = full[:, f * levels:(f + 1) * levels] / divisor


def kernel_out(devices, capacity, recv_ref, out_hbm, out_ref, sem):
    values = out_ref.shape[0]
    block = values // sem.shape[0]
    pitch = recv_ref.shape[0] // devices
    copies = []
    for step, at in enumerate(range(0, values, block)):
        first = step * capacity
        ranked = [recv_ref[pl.ds(first + r, devices, stride=pitch), :] for r in range(capacity)]
        out_ref[at:at + block, :] = jnp.concatenate(ranked, axis=0).T
        part = pl.ds(at, block)
        copies.append(fetch(out_ref.at[part], out_hbm.at[part], sem.at[step]))
    for copy in copies:
        copy.wait()


def params(mib):
    return pltpu.CompilerParams(vmem_limit_bytes=mib * MIB)


def cost(flops, byte_count):
    return pl.CostEstimate(flops=flops, bytes_accessed=byte_count, transcendentals=0)


def shift(face, axis, by):
    count = lax.axis_size(axis)
    return lax.ppermute(face, axis, [(i, (i + by) % count) for i in range(count)])


def body(crm_state, gcm_state, mass, dest, cost_class):
    devices = lax.axis_size(("ex", "ey"))
    field_count, levels, width, owned = crm_state.shape
    elx, ely, side = gcm_state.shape[2:5]
    capacity = max(2, 2 * owned // devices)
    slots = capacity * devices
    values = field_count * levels * width
    f32 = jnp.float32
    gcm_nodes = gcm_state.transpose(0, 2, 3, 4, 5, 1).reshape(field_count, owned, levels)
    mass_nodes = mass.transpose(1, 2, 3, 4, 0).reshape(owned, levels)
    packed = (devices, values // owned * capacity, owned)
    sizes = (elx, ely, side)
    face_x = jax.ShapeDtypeStruct((ely * side, owned), f32)
    face_y = jax.ShapeDtypeStruct((elx * side, owned), f32)
    in_hbm = pl.BlockSpec(memory_space=pltpu.HBM)
    in_vmem = pl.BlockSpec(memory_space=pltpu.VMEM)
    square = jax.ShapeDtypeStruct((owned, owned), f32)
    send, nodes, low, high = pl.pallas_call(
        functools.partial(kernel_a, devices, capacity, *sizes),
        out_shape=(jax.ShapeDtypeStruct(packed, f32), square, face_x, face_x),
        in_specs=[in_hbm] * 5,
        out_specs=(in_hbm, in_vmem, in_vmem, in_vmem),
        scratch_shapes=[
            pltpu.VMEM(crm_state.shape, f32),
            pltpu.VMEM(crm_state.shape, f32),
            pltpu.VMEM((owned, owned), f32),
            pltpu.VMEM((owned, owned), f32),
            pltpu.VMEM(crm_state.shape, f32),
            pltpu.VMEM(gcm_nodes.shape, f32),
            pltpu.VMEM(mass_nodes.shape, f32),
            pltpu.VMEM((1, owned), jnp.int32),
            pltpu.VMEM((1, owned), jnp.int32),
            pltpu.VMEM(packed, f32),
            pltpu.SemaphoreType.DMA((4,)),
            pltpu.SemaphoreType.DMA((levels * width // owned,)),
            pltpu.SemaphoreType.DMA((field_count,)),
        ],
        compiler_params=params(63),
        name="cloud_models",
    )(crm_state, gcm_nodes, mass_nodes, dest.reshape(1, owned), cost_class.reshape(1, owned))
    received = lax.all_to_all(
        send, ("ex", "ey"), split_axis=0, concat_axis=0, tiled=True
    )
    east = shift(low, "ex", -1)
    west = shift(high, "ex", 1)
    summed, low, high = pl.pallas_call(
        functools.partial(kernel_x, *sizes),
        out_shape=(square, face_y, face_y),
        compiler_params=params(8),
        cost_estimate=cost(10**5, 10**5),
        name="edge_sum_first",
    )(nodes, west, east)
    north = shift(low, "ey", -1)
    south = shift(high, "ey", 1)
    gcm_out = pl.pallas_call(
        functools.partial(kernel_y, *sizes),
        out_shape=jax.ShapeDtypeStruct((field_count, owned, levels), f32),
        scratch_shapes=[pltpu.VMEM((owned, owned), f32)],
        compiler_params=params(8),
        cost_estimate=cost(10**5, 10**5),
        name="edge_sum_second",
    )(summed, south, north)
    gcm_out = gcm_out.reshape(field_count, elx, ely, side, side, levels).transpose(0, 5, 1, 2, 3, 4)
    cloud = pl.pallas_call(
        functools.partial(kernel_out, devices, capacity),
        in_specs=[in_vmem],
        out_specs=in_hbm,
        out_shape=jax.ShapeDtypeStruct((values, slots), f32),
        scratch_shapes=[pltpu.VMEM((values, slots), f32), pltpu.SemaphoreType.DMA((values // owned,))],
        compiler_params=params(16),
        name="cloud_slots",
    )(received.reshape(-1, owned))
    return cloud.reshape(field_count, levels, width, slots), gcm_out


def solution(mesh):
    return jax.shard_map(
        body,
        mesh=mesh,
        in_specs=(
            P(None, None, None, ("ex", "ey")),
            P(None, None, "ex", "ey", None, None),
            P(None, "ex", "ey", None, None),
            P(("ex", "ey"), None),
            P(("ex", "ey")),
        ),
        out_specs=(P(None, None, None, ("ex", "ey")), P(None, None, "ex", "ey", None, None)),
        check_vma=False,
    )
```

```python
import functools

import jax
import jax.numpy as jnp
from jax import lax
from jax.experimental import pallas as pl
from jax.experimental.pallas import tpu as pltpu
from jax.sharding import PartitionSpec as P

diffusion = 0.1
advection = 0.15
buoyancy = 0.3
latent_heat = 0.5
fallout = 0.2
condense_rate = 0.4
nudging = 0.5

NT = (((1,), (1,)), ((), ()))
MIB = 1024 * 1024


def substep_level(values_at, profile_row, z, levels, field_count, active):
    values = [values_at(f, z) for f in range(field_count)]
    width = values[0].shape[0]
    x_wind = values[0]
    condensed = condense_rate * jnp.maximum(values[3], 0.0)
    drift = (advection * 0.5) * x_wind
    results = []
    for f in range(field_count):
        v = values[f]
        east = pltpu.roll(v, width - 1, 0)
        west = pltpu.roll(v, 1, 0)
        around = east + west
        if z + 1 < levels:
            around = around + values_at(f, z + 1)
        if z > 0:
            around = around + values_at(f, z - 1)
        mean = jnp.sum(v, axis=0, keepdims=True) * (1.0 / width)
        nudged = nudging * (profile_row(f, z) - mean)
        change = diffusion * (around - 4.0 * v) - drift * (east - west) + nudged
        if f == 1:
            change = change + buoyancy * values[2]
        elif f == 2:
            change = change - buoyancy * values[1] + latent_heat * condensed
        elif f == 3:
            change = change - condensed
        elif f == 4:
            change = change + condensed - fallout * v
        results.append(jnp.where(active, v + change, v))
    return results


def fetch(source, target, sem):
    copy = pltpu.make_async_copy(source, target, sem)
    copy.start()
    return copy


def cloud_kernel(devices, capacity, crm_hbm, gcm_hbm, mass_hbm, dest_hbm, cost_hbm,
                 send_hbm, nodes_ref, low_ref, high_ref, first_ref, second_ref, prof_ref, tend_ref,
                 crm_ref, gcm_ref, mass_ref, dest_ref, cost_ref, send_ref, small_sem, crm_sem, send_sem):
    field_count, levels, width, owned = crm_ref.shape
    small = [
        fetch(gcm_hbm, gcm_ref, small_sem.at[0]),
        fetch(mass_hbm, mass_ref, small_sem.at[1]),
        fetch(dest_hbm, dest_ref, small_sem.at[2]),
        fetch(cost_hbm, cost_ref, small_sem.at[3]),
    ]
    group = owned // width
    pieces = [
        fetch(crm_hbm.at[:, pl.ds(z, group)], crm_ref.at[:, pl.ds(z, group)], crm_sem.at[z // group])
        for z in range(0, levels, group)
    ]
    for copy in small:
        copy.wait()
    used = field_count * levels
    total = used + levels
    nodes = gcm_ref.shape[1]
    mass = mass_ref[...]
    spare = nodes - total
    grid_fields = jnp.concatenate(
        [gcm_ref[f] for f in range(field_count)] + [mass, jnp.zeros((nodes, spare), jnp.float32)], axis=1
    )
    prof_ref[...] = grid_fields.T
    tend_ref[...] = jnp.zeros_like(tend_ref)
    cost = cost_ref[...]
    once = jnp.broadcast_to(cost >= 1, (width, owned))
    twice = jnp.broadcast_to(cost >= 2, (width, owned))

    def profile_row(f, z):
        return prof_ref[pl.ds(f * levels + z, 1), :]

    for z in range(levels):
        if z == 0:
            pieces[0].wait()
        if (z + 1) % group == 0 and z + 1 < levels:
            pieces[(z + 1) // group].wait()
        fresh = substep_level(lambda f, k: crm_ref[f, k], profile_row, z, levels, field_count, once)
        for f in range(field_count):
            first_ref[f, z] = fresh[f]
    for z in range(levels):
        fresh = substep_level(lambda f, k: first_ref[f, k], profile_row, z, levels, field_count, twice)
        for f in range(field_count):
            second_ref[f, z] = fresh[f]
            gained = jnp.sum(fresh[f] - crm_ref[f, z], axis=0, keepdims=True) * (1.0 / width)
            tend_ref[pl.ds(f * levels + z, 1), :] = gained

    dest_row = jnp.broadcast_to(dest_ref[...].astype(jnp.float32), (owned, owned))
    dest_col = dest_row.T
    rows = lax.broadcasted_iota(jnp.int32, (owned, owned), 0)
    cols = lax.broadcasted_iota(jnp.int32, (owned, owned), 1)
    earlier = jnp.where((dest_row == dest_col) & (rows < cols), 1, 0)
    rank = jnp.sum(earlier, axis=0, keepdims=True)
    slot = dest_ref[...] * capacity + rank
    slots = devices * capacity
    slot_rows = lax.broadcasted_iota(jnp.int32, (slots, owned), 0)
    picks = jnp.where(slot_rows == slot, 1.0, 0.0).astype(jnp.bfloat16)

    field_rows = levels // group * capacity
    aligned = field_rows % 8 == 0
    sends = []
    for f in range(field_count):
        for z in range(0, levels, group):
            block = second_ref[f, pl.ds(z, group)].reshape(group * width, owned)
            high = block.astype(jnp.bfloat16)
            rest = block - high.astype(jnp.float32)
            middle = rest.astype(jnp.bfloat16)
            low = (rest - middle.astype(jnp.float32)).astype(jnp.bfloat16)
            moved = lax.dot_general(picks, high, NT, preferred_element_type=jnp.float32)
            moved = moved + lax.dot_general(picks, middle, NT, preferred_element_type=jnp.float32)
            moved = moved + lax.dot_general(picks, low, NT, preferred_element_type=jnp.float32)
            at = (f * levels + z) // group * capacity
            send_ref[:, at:at + capacity, :] = moved.reshape(devices, capacity, group * width)
        if aligned:
            part = pl.ds(f * field_rows, field_rows)
            sends.append(fetch(send_ref.at[:, part], send_hbm.at[:, part], send_sem.at[f]))
    if not aligned:
        sends.append(fetch(send_ref, send_hbm, send_sem.at[0]))

    factors = jnp.concatenate(
        [mass] * field_count + [jnp.ones((nodes, nodes - used), jnp.float32)], axis=1
    )
    weighted = (grid_fields + tend_ref[...].T) * factors
    nodes_ref[...] = weighted
    return sends


def edges_y(elx, ely, side, nodes_ref, low_ref, high_ref):
    step = side * side
    for a in range(elx):
        first = a * ely * step
        final = (a * ely + ely - 1) * step + side - 1
        low_ref[a * side:(a + 1) * side, :] = nodes_ref[pl.ds(first, side, stride=side), :]
        high_ref[a * side:(a + 1) * side, :] = nodes_ref[pl.ds(final, side, stride=side), :]


def kernel_a(devices, capacity, elx, ely, side, *refs):
    sends = cloud_kernel(devices, capacity, *refs)
    edges_y(elx, ely, side, *refs[6:9])
    for copy in sends:
        copy.wait()


def kernel_y(elx, ely, side, nodes_ref, south_ref, north_ref, sum_ref, low_ref, high_ref):
    step = side * side
    sum_ref[...] = nodes_ref[...]
    for a in range(elx):
        for b in range(ely):
            base = (a * ely + b) * step
            if b > 0:
                gain = nodes_ref[pl.ds(base - step + side - 1, side, stride=side), :]
            else:
                gain = south_ref[a * side:(a + 1) * side, :]
            here = pl.ds(base, side, stride=side)
            sum_ref[here, :] = nodes_ref[here, :] + gain
            if b + 1 < ely:
                gain = nodes_ref[pl.ds(base + step, side, stride=side), :]
            else:
                gain = north_ref[a * side:(a + 1) * side, :]
            here = pl.ds(base + side - 1, side, stride=side)
            sum_ref[here, :] = nodes_ref[here, :] + gain
    for b in range(ely):
        low_ref[b * side:(b + 1) * side, :] = sum_ref[b * step:b * step + side, :]
        start = (elx - 1) * ely * step + b * step + (side - 1) * side
        high_ref[b * side:(b + 1) * side, :] = sum_ref[start:start + side, :]


def kernel_x(elx, ely, side, sum_ref, west_ref, east_ref, out_ref, full_ref):
    step = side * side
    field_count, nodes, levels = out_ref.shape
    full_ref[...] = sum_ref[...]
    for a in range(elx):
        for b in range(ely):
            base = (a * ely + b) * step
            last = base + (side - 1) * side
            if a > 0:
                before = ((a - 1) * ely + b) * step + (side - 1) * side
                gain = sum_ref[before:before + side, :]
            else:
                gain = west_ref[b * side:(b + 1) * side, :]
            full_ref[base:base + side, :] = sum_ref[base:base + side, :] + gain
            if a + 1 < elx:
                after = ((a + 1) * ely + b) * step
                gain = sum_ref[after:after + side, :]
            else:
                gain = east_ref[b * side:(b + 1) * side, :]
            full_ref[last:last + side, :] = sum_ref[last:last + side, :] + gain
    full = full_ref[...]
    divisor = full[:, field_count * levels:(field_count + 1) * levels]
    for f in range(field_count):
        out_ref[f] = full[:, f * levels:(f + 1) * levels] / divisor


def kernel_out(devices, capacity, recv_ref, out_hbm, out_ref, sem):
    values = out_ref.shape[0]
    block = values // sem.shape[0]
    pitch = recv_ref.shape[0] // devices
    copies = []
    for step, at in enumerate(range(0, values, block)):
        first = step * capacity
        ranked = [recv_ref[pl.ds(first + r, devices, stride=pitch), :] for r in range(capacity)]
        out_ref[at:at + block, :] = jnp.concatenate(ranked, axis=0).T
        part = pl.ds(at, block)
        copies.append(fetch(out_ref.at[part], out_hbm.at[part], sem.at[step]))
    for copy in copies:
        copy.wait()


def params(mib):
    return pltpu.CompilerParams(vmem_limit_bytes=mib * MIB)


def cost(flops, byte_count):
    return pl.CostEstimate(flops=flops, bytes_accessed=byte_count, transcendentals=0)


def shift(face, axis, by):
    count = lax.axis_size(axis)
    return lax.ppermute(face, axis, [(i, (i + by) % count) for i in range(count)])


def body(crm_state, gcm_state, mass, dest, cost_class):
    devices = lax.axis_size(("ex", "ey"))
    field_count, levels, width, owned = crm_state.shape
    elx, ely, side = gcm_state.shape[2:5]
    capacity = max(2, 2 * owned // devices)
    slots = capacity * devices
    values = field_count * levels * width
    f32 = jnp.float32
    gcm_nodes = gcm_state.transpose(0, 2, 3, 4, 5, 1).reshape(field_count, owned, levels)
    mass_nodes = mass.transpose(1, 2, 3, 4, 0).reshape(owned, levels)
    packed = (devices, values // owned * capacity, owned)
    sizes = (elx, ely, side)
    face_x = jax.ShapeDtypeStruct((ely * side, owned), f32)
    face_y = jax.ShapeDtypeStruct((elx * side, owned), f32)
    in_hbm = pl.BlockSpec(memory_space=pltpu.HBM)
    in_vmem = pl.BlockSpec(memory_space=pltpu.VMEM)
    square = jax.ShapeDtypeStruct((owned, owned), f32)
    send, nodes, low, high = pl.pallas_call(
        functools.partial(kernel_a, devices, capacity, *sizes),
        out_shape=(jax.ShapeDtypeStruct(packed, f32), square, face_y, face_y),
        in_specs=[in_hbm] * 5,
        out_specs=(in_hbm, in_vmem, in_vmem, in_vmem),
        scratch_shapes=[
            pltpu.VMEM(crm_state.shape, f32),
            pltpu.VMEM(crm_state.shape, f32),
            pltpu.VMEM((owned, owned), f32),
            pltpu.VMEM((owned, owned), f32),
            pltpu.VMEM(crm_state.shape, f32),
            pltpu.VMEM(gcm_nodes.shape, f32),
            pltpu.VMEM(mass_nodes.shape, f32),
            pltpu.VMEM((1, owned), jnp.int32),
            pltpu.VMEM((1, owned), jnp.int32),
            pltpu.VMEM(packed, f32),
            pltpu.SemaphoreType.DMA((4,)),
            pltpu.SemaphoreType.DMA((levels * width // owned,)),
            pltpu.SemaphoreType.DMA((field_count,)),
        ],
        compiler_params=params(63),
        name="cloud_models",
    )(crm_state, gcm_nodes, mass_nodes, dest.reshape(1, owned), cost_class.reshape(1, owned))
    received = lax.all_to_all(
        send, ("ex", "ey"), split_axis=0, concat_axis=0, tiled=True
    )
    north = shift(low, "ey", -1)
    south = shift(high, "ey", 1)
    summed, low, high = pl.pallas_call(
        functools.partial(kernel_y, *sizes),
        out_shape=(square, face_x, face_x),
        compiler_params=params(8),
        cost_estimate=cost(10**5, 10**5),
        name="edge_sum_second",
    )(nodes, south, north)
    east = shift(low, "ex", -1)
    west = shift(high, "ex", 1)
    gcm_out = pl.pallas_call(
        functools.partial(kernel_x, *sizes),
        out_shape=jax.ShapeDtypeStruct((field_count, owned, levels), f32),
        scratch_shapes=[pltpu.VMEM((owned, owned), f32)],
        compiler_params=params(8),
        cost_estimate=cost(10**5, 10**5),
        name="edge_sum_first",
    )(summed, west, east)
    gcm_out = gcm_out.reshape(field_count, elx, ely, side, side, levels).transpose(0, 5, 1, 2, 3, 4)
    cloud = pl.pallas_call(
        functools.partial(kernel_out, devices, capacity),
        in_specs=[in_vmem],
        out_specs=in_hbm,
        out_shape=jax.ShapeDtypeStruct((values, slots), f32),
        scratch_shapes=[pltpu.VMEM((values, slots), f32), pltpu.SemaphoreType.DMA((values // owned,))],
        compiler_params=params(16),
        name="cloud_slots",
    )(received.reshape(-1, owned))
    return cloud.reshape(field_count, levels, width, slots), gcm_out


def solution(mesh):
    return jax.shard_map(
        body,
        mesh=mesh,
        in_specs=(
            P(None, None, None, ("ex", "ey")),
            P(None, None, "ex", "ey", None, None),
            P(None, "ex", "ey", None, None),
            P(("ex", "ey"), None),
            P(("ex", "ey")),
        ),
        out_specs=(P(None, None, None, ("ex", "ey")), P(None, None, "ex", "ey", None, None)),
        check_vma=False,
    )
```

```python
import functools

import jax
import jax.numpy as jnp
from jax import lax
from jax.experimental import pallas as pl
from jax.experimental.pallas import tpu as pltpu
from jax.sharding import PartitionSpec as P

diffusion = 0.1
advection = 0.15
buoyancy = 0.3
latent_heat = 0.5
fallout = 0.2
condense_rate = 0.4
nudging = 0.5

AXES = ("ex", "ey")
NT = (((1,), (1,)), ((), ()))
MIB = 1024 * 1024
REGROUP_FLOPS = 6*10**9
EDGE_FLOPS = 10**5
EARLY_BLOCKS = 2
EARLY_FLOPS = 13*10**9


def substep_level(values_at, nudge_row, z, levels, field_count, active=None):
    values = [values_at(f, z) for f in range(field_count)]
    width = values[0].shape[0]
    drift = (advection * 0.5) * values[0]
    from_east, from_west = diffusion - drift, diffusion + drift
    condensed = condense_rate * jnp.maximum(values[3], 0.0)
    results = []
    for f in range(field_count):
        v = values[f]
        east = pltpu.roll(v, width - 1, 0)
        west = pltpu.roll(v, 1, 0)
        fresh = east * from_east + west * from_west
        if 0 < z < levels - 1:
            fresh = fresh + diffusion * (values_at(f, z + 1) + values_at(f, z - 1))
        else:
            fresh = fresh + diffusion * values_at(f, z + 1 if z == 0 else z - 1)
        fresh = fresh + (nudge_row(f, z) - (nudging / width) * jnp.sum(v, axis=0, keepdims=True))
        own = 1.0 - 4.0 * diffusion
        if f == 1:
            fresh = fresh + buoyancy * values[2]
        elif f == 2:
            fresh = fresh - buoyancy * values[1] + latent_heat * condensed
        elif f == 3:
            fresh = fresh - condensed
        elif f == 4:
            fresh = fresh + condensed
            own = own - fallout
        fresh = fresh + own * v
        results.append(fresh if active is None else jnp.where(active, fresh, v))
    return results


def slot_rank(dest):
    owned = dest.shape[1]
    named = jnp.broadcast_to(dest.astype(jnp.float32), (owned, owned))
    rows = lax.broadcasted_iota(jnp.int32, (owned, owned), 0)
    cols = lax.broadcasted_iota(jnp.int32, (owned, owned), 1)
    earlier = jnp.where((named == named.T) & (rows < cols), 1, 0)
    return jnp.sum(earlier, axis=0, keepdims=True)


def one_hot_rows(slot, count):
    rows = lax.broadcasted_iota(jnp.int32, (count, slot.shape[1]), 0)
    return jnp.concatenate([jnp.where(rows == slot, 1.0, 0.0).astype(jnp.bfloat16)] * 3, axis=1)


def hop_bits(devices):
    bits = devices.bit_length() - 1
    return [bits - 1] + list(range(bits - 1))


def hop_order(difference, devices):
    place = jnp.zeros_like(difference)
    for bit in hop_bits(devices):
        place = 2 * place + ((difference >> bit) & 1)
    return place


def picked(picks, block):
    high = block.astype(jnp.bfloat16)
    rest = block - high.astype(jnp.float32)
    middle = rest.astype(jnp.bfloat16)
    low = (rest - middle.astype(jnp.float32)).astype(jnp.bfloat16)
    parts = jnp.concatenate([high, middle, low], axis=1)
    return lax.dot_general(picks, parts, NT, preferred_element_type=jnp.float32)


def fetch(source, target, sem):
    copy = pltpu.make_async_copy(source, target, sem)
    copy.start()
    return copy


def cloud_kernel(devices, capacity, early, me_ref, crm_hbm, gcm_hbm, mass_hbm, dest_hbm, cost_hbm,
                 send_hbm, far_hbm, near_hbm, nodes_ref, low_ref, high_ref, first_ref, second_ref, prof_ref, tend_ref,
                 crm_ref, gcm_ref, mass_ref, dest_ref, cost_ref, send_ref, early_ref, small_sem, crm_sem, send_sem, early_sem):
    field_count, levels, width, owned = crm_ref.shape
    group = owned // width
    small = [
        fetch(dest_hbm, dest_ref, small_sem.at[0]),
        fetch(gcm_hbm, gcm_ref, small_sem.at[1]),
        fetch(cost_hbm, cost_ref, small_sem.at[2]),
    ]
    pieces = [
        fetch(crm_hbm.at[:, pl.ds(z, group)], crm_ref.at[:, pl.ds(z, group)], crm_sem.at[z // group])
        for z in range(0, levels, group)
    ]
    small.append(fetch(mass_hbm, mass_ref, small_sem.at[3]))
    used = field_count * levels
    nodes = gcm_ref.shape[1]

    small[0].wait()
    rank = slot_rank(dest_ref[...])
    picks = one_hot_rows(dest_ref[...] * capacity + rank, devices * capacity)
    if early:
        turned = hop_order(dest_ref[...] ^ me_ref[0], devices)
        early_picks = one_hot_rows(turned * capacity + rank, devices * capacity)
    small[1].wait()
    grid_fields = jnp.concatenate(
        [gcm_ref[f] for f in range(field_count)] + [jnp.zeros((nodes, nodes - used), jnp.float32)], axis=1
    )
    prof_ref[...] = nudging * grid_fields.T
    small[2].wait()
    twice = jnp.broadcast_to(cost_ref[...] >= 2, (width, owned))

    def nudge_row(f, z):
        return prof_ref[pl.ds(f * levels + z, 1), :]

    def first_substep(z):
        fresh = substep_level(lambda f, k: crm_ref[f, k], nudge_row, z, levels, field_count)
        for f in range(field_count):
            first_ref[f, z] = fresh[f]

    def second_substep(z):
        fresh = substep_level(lambda f, k: first_ref[f, k], nudge_row, z, levels, field_count, twice)
        for f in range(field_count):
            second_ref[f, z] = fresh[f]

    pieces[0].wait()
    for z in range(levels):
        if (z + 1) % group == 0 and z + 1 < levels:
            pieces[(z + 1) // group].wait()
        first_substep(z)
    for z in range(levels):
        second_substep(z)

    sends = []
    if early:
        first = levels // group - 1
        at = field_count - early
        block = second_ref[pl.ds(at, early), pl.ds(first * group, group)].reshape(early * group * width, owned)
        moved = picked(early_picks, block)
        for e in range(early):
            rows = moved[:, e * owned:(e + 1) * owned].reshape(devices, capacity, owned)
            early_ref[:, e * capacity:(e + 1) * capacity, :] = rows
        half = devices // 2
        sends.append(fetch(early_ref.at[pl.ds(half, half)], far_hbm, early_sem.at[0]))
        sends.append(fetch(early_ref.at[pl.ds(0, half)], near_hbm, early_sem.at[1]))
    group_rows = field_count * capacity
    aligned = group_rows % 8 == 0
    for number in range(levels // group):
        held = field_count - (early if number == levels // group - 1 else 0)
        blocks = second_ref[pl.ds(0, held), pl.ds(number * group, group)].reshape(held * group * width, owned)
        moved = picked(picks, blocks)
        for f in range(held):
            at = (number * field_count + f) * capacity
            send_ref[:, at:at + capacity, :] = moved[:, f * owned:(f + 1) * owned].reshape(devices, capacity, owned)
        if aligned:
            part = pl.ds(number * group_rows, held * capacity)
            sends.append(fetch(send_ref.at[:, part], send_hbm.at[:, part], send_sem.at[number]))
    if not aligned:
        sends.append(fetch(send_ref, send_hbm, send_sem.at[0]))

    tend_ref[...] = jnp.zeros_like(tend_ref)
    for f in range(field_count):
        for z in range(levels):
            gained = jnp.sum(second_ref[f, z] - crm_ref[f, z], axis=0, keepdims=True) * (1.0 / width)
            tend_ref[pl.ds(f * levels + z, 1), :] = gained
    small[3].wait()
    mass = mass_ref[...]
    fields = jnp.concatenate(
        [gcm_ref[f] for f in range(field_count)] + [mass, jnp.zeros((nodes, nodes - used - levels), jnp.float32)],
        axis=1,
    )
    factors = jnp.concatenate([mass] * field_count + [jnp.ones((nodes, nodes - used), jnp.float32)], axis=1)
    nodes_ref[...] = (fields + tend_ref[...].T) * factors
    return sends


def edges_y(elx, ely, side, nodes_ref, low_ref, high_ref):
    step = side * side
    for a in range(elx):
        first = a * ely * step
        final = (a * ely + ely - 1) * step + side - 1
        low_ref[a * side:(a + 1) * side, :] = nodes_ref[pl.ds(first, side, stride=side), :]
        high_ref[a * side:(a + 1) * side, :] = nodes_ref[pl.ds(final, side, stride=side), :]


def kernel_a(devices, capacity, early, elx, ely, side, *refs):
    sends = cloud_kernel(devices, capacity, early, *refs)
    edges_y(elx, ely, side, *refs[9:12])
    for copy in sends:
        copy.wait()


def kernel_y(elx, ely, side, nodes_ref, south_ref, north_ref, sum_ref, low_ref, high_ref):
    step = side * side
    sum_ref[...] = nodes_ref[...]
    for a in range(elx):
        for b in range(ely):
            base = (a * ely + b) * step
            if b > 0:
                gain = nodes_ref[pl.ds(base - step + side - 1, side, stride=side), :]
            else:
                gain = south_ref[a * side:(a + 1) * side, :]
            here = pl.ds(base, side, stride=side)
            sum_ref[here, :] = nodes_ref[here, :] + gain
            if b + 1 < ely:
                gain = nodes_ref[pl.ds(base + step, side, stride=side), :]
            else:
                gain = north_ref[a * side:(a + 1) * side, :]
            here = pl.ds(base + side - 1, side, stride=side)
            sum_ref[here, :] = nodes_ref[here, :] + gain
    for b in range(ely):
        low_ref[b * side:(b + 1) * side, :] = sum_ref[b * step:b * step + side, :]
        start = (elx - 1) * ely * step + b * step + (side - 1) * side
        high_ref[b * side:(b + 1) * side, :] = sum_ref[start:start + side, :]


def kernel_x(elx, ely, side, sum_ref, west_ref, east_ref, out_ref, full_ref):
    step = side * side
    field_count, nodes, levels = out_ref.shape
    full_ref[...] = sum_ref[...]
    for a in range(elx):
        for b in range(ely):
            base = (a * ely + b) * step
            last = base + (side - 1) * side
            if a > 0:
                before = ((a - 1) * ely + b) * step + (side - 1) * side
                gain = sum_ref[before:before + side, :]
            else:
                gain = west_ref[b * side:(b + 1) * side, :]
            full_ref[base:base + side, :] = sum_ref[base:base + side, :] + gain
            if a + 1 < elx:
                after = ((a + 1) * ely + b) * step
                gain = sum_ref[after:after + side, :]
            else:
                gain = east_ref[b * side:(b + 1) * side, :]
            full_ref[last:last + side, :] = sum_ref[last:last + side, :] + gain
    full = full_ref[...]
    divisor = full[:, field_count * levels:(field_count + 1) * levels]
    for f in range(field_count):
        out_ref[f] = full[:, f * levels:(f + 1) * levels] / divisor


def turned_blocks(rows_of, out_hbm, out_ref, sem):
    block = out_ref.shape[0] // len(rows_of)
    copies = []
    for number, (step, slots_at) in enumerate(rows_of):
        here, there = pl.ds(number * block, block), pl.ds(step * block, block)
        out_ref[here, :] = slots_at().T
        copies.append(fetch(out_ref.at[here], out_hbm.at[there], sem.at[number]))
    for copy in copies:
        copy.wait()


def kernel_out(devices, capacity, groups, field_count, early, recv_ref, *refs):
    out_hbm, out_ref, sem = refs[-3:]
    pitch = recv_ref.shape[0] // devices

    def rows(first):
        ranked = [recv_ref[pl.ds(first + r, devices, stride=pitch), :] for r in range(capacity)]
        return jnp.concatenate(ranked, axis=0)

    blocks = groups * field_count - early
    steps = [(at % field_count) * groups + at // field_count for at in range(blocks)]
    rows_of = [(step, functools.partial(rows, at * capacity)) for at, step in enumerate(steps)]
    turned_blocks(rows_of, out_hbm, out_ref, sem)


def kernel_early(devices, capacity, groups, field_count, early, sources, me_ref, kept_ref, last_ref,
                 out_hbm, row_ref, out_ref, sem):
    slots = devices * capacity
    arrived = [(ref, index) for ref in (kept_ref, last_ref) for index in range(devices // 2)]
    for (ref, index), bits in zip(arrived, sources):
        for e in range(early):
            tile = ref[index, pl.ds(e * capacity, capacity), :]
            row_ref[pl.ds(e * slots + (me_ref[0] ^ bits), capacity, stride=devices), :] = tile
    steps = [(field_count - early + e) * groups + groups - 1 for e in range(early)]
    rows_of = [(step, lambda e=e: row_ref[e * slots:(e + 1) * slots, :]) for e, step in enumerate(steps)]
    turned_blocks(rows_of, out_hbm, out_ref, sem)


def params(mib):
    return pltpu.CompilerParams(vmem_limit_bytes=mib * MIB)


def cost(flops, byte_count):
    return pl.CostEstimate(flops=flops, bytes_accessed=byte_count, transcendentals=0)


def shift(face, axis, by):
    count = lax.axis_size(axis)
    return lax.ppermute(face, axis, [(i, (i + by) % count) for i in range(count)])


def exchange(block, bits):
    count = lax.axis_size(AXES)
    return lax.ppermute(block, AXES, [(i, i ^ bits) for i in range(count)])


def kernel_regroup(kept_ref, last_ref, keep_ref, pass_ref):
    half = kept_ref.shape[1] // 2
    keep_ref[0:1] = kept_ref[:, 0:half]
    keep_ref[1:2] = last_ref[:, 0:half]
    pass_ref[0:1] = kept_ref[:, half:]
    pass_ref[1:2] = last_ref[:, half:]


def regrouped(kept, last, first):
    half = kept.shape[1] // 2
    if first:
        shape = jax.ShapeDtypeStruct((2, half) + kept.shape[2:], kept.dtype)
        return pl.pallas_call(
            kernel_regroup,
            out_shape=(shape, shape),
            compiler_params=params(8),
            cost_estimate=cost(REGROUP_FLOPS, 10**6),
            name="regroup",
        )(kept, last)
    passed = jnp.concatenate([kept[:, half:], last[:, half:]])
    return jnp.concatenate([kept[:, :half], last[:, :half]]), passed


def hops(near, far, devices):
    first, *others = hop_bits(devices)
    kept, last = near[None], exchange(far, 1 << first)[None]
    kept_from, last_from = [0], [1 << first]
    for bit in others:
        kept, passed = regrouped(kept, last, bit == others[0])
        last = exchange(passed, 1 << bit)
        kept_from = kept_from + last_from
        last_from = [source ^ (1 << bit) for source in kept_from]
    return kept[:, 0], last[:, 0], kept_from + last_from


def body(crm_state, gcm_state, mass, dest, cost_class):
    devices = lax.axis_size(("ex", "ey"))
    field_count, levels, width, owned = crm_state.shape
    elx, ely, side = gcm_state.shape[2:5]
    capacity = max(2, 2 * owned // devices)
    slots = capacity * devices
    values = field_count * levels * width
    f32 = jnp.float32
    gcm_nodes = gcm_state.transpose(0, 2, 3, 4, 5, 1).reshape(field_count, owned, levels)
    mass_nodes = mass.transpose(1, 2, 3, 4, 0).reshape(owned, levels)
    sizes = (elx, ely, side)
    face_x = jax.ShapeDtypeStruct((ely * side, owned), f32)
    face_y = jax.ShapeDtypeStruct((elx * side, owned), f32)
    in_hbm = pl.BlockSpec(memory_space=pltpu.HBM)
    in_vmem = pl.BlockSpec(memory_space=pltpu.VMEM)
    square = jax.ShapeDtypeStruct((owned, owned), f32)
    in_smem = pl.BlockSpec(memory_space=pltpu.SMEM)
    me = lax.axis_index(AXES).astype(jnp.int32).reshape(1)
    groups = levels * width // owned
    early = EARLY_BLOCKS if capacity % 8 == 0 and devices & (devices - 1) == 0 else 0
    packed = (devices, (values // owned - early) * capacity, owned)
    apart = (max(2, devices) // 2, max(1, early) * capacity, owned)
    send, far, near, nodes, low, high = pl.pallas_call(
        functools.partial(kernel_a, devices, capacity, early, *sizes),
        out_shape=(
            jax.ShapeDtypeStruct(packed, f32),
            jax.ShapeDtypeStruct(apart, f32),
            jax.ShapeDtypeStruct(apart, f32),
            square,
            face_y,
            face_y,
        ),
        in_specs=[in_smem] + [in_hbm] * 5,
        out_specs=(in_hbm, in_hbm, in_hbm, in_vmem, in_vmem, in_vmem),
        scratch_shapes=[
            pltpu.VMEM(crm_state.shape, f32),
            pltpu.VMEM(crm_state.shape, f32),
            pltpu.VMEM((owned, owned), f32),
            pltpu.VMEM((owned, owned), f32),
            pltpu.VMEM(crm_state.shape, f32),
            pltpu.VMEM(gcm_nodes.shape, f32),
            pltpu.VMEM(mass_nodes.shape, f32),
            pltpu.VMEM((1, owned), jnp.int32),
            pltpu.VMEM((1, owned), jnp.int32),
            pltpu.VMEM(packed, f32),
            pltpu.VMEM((devices,) + apart[1:], f32),
            pltpu.SemaphoreType.DMA((4,)),
            pltpu.SemaphoreType.DMA((groups,)),
            pltpu.SemaphoreType.DMA((groups,)),
            pltpu.SemaphoreType.DMA((2,)),
        ],
        compiler_params=params(63),
        name="cloud_models",
    )(me, crm_state, gcm_nodes, mass_nodes, dest.reshape(1, owned), cost_class.reshape(1, owned))
    received = lax.all_to_all(send, AXES, split_axis=0, concat_axis=0, tiled=True)
    if early:
        kept, last, sources = hops(near, far, devices)
    north = shift(low, "ey", -1)
    south = shift(high, "ey", 1)
    summed, low, high = pl.pallas_call(
        functools.partial(kernel_y, *sizes),
        out_shape=(square, face_x, face_x),
        compiler_params=params(8),
        cost_estimate=cost(10**5, 10**5),
        name="edge_sum_second",
    )(nodes, south, north)
    east = shift(low, "ex", -1)
    west = shift(high, "ex", 1)
    if early:
        summed, last = lax.optimization_barrier((summed, last))
    gcm_out = pl.pallas_call(
        functools.partial(kernel_x, *sizes),
        out_shape=jax.ShapeDtypeStruct((field_count, owned, levels), f32),
        scratch_shapes=[pltpu.VMEM((owned, owned), f32)],
        compiler_params=params(8),
        cost_estimate=cost(EDGE_FLOPS, 10**5),
        name="edge_sum_first",
    )(summed, west, east)
    gcm_out = gcm_out.reshape(field_count, elx, ely, side, side, levels).transpose(0, 5, 1, 2, 3, 4)
    out_shape = jax.ShapeDtypeStruct((values, slots), f32)
    block_count = values // owned
    begun = []
    if early:
        begun.append(pl.pallas_call(
            functools.partial(kernel_early, devices, capacity, groups, field_count, early, sources),
            in_specs=[in_smem, in_vmem, in_vmem],
            out_specs=in_hbm,
            out_shape=out_shape,
            scratch_shapes=[
                pltpu.VMEM((early * slots, owned), f32),
                pltpu.VMEM((early * owned, slots), f32),
                pltpu.SemaphoreType.DMA((early,)),
            ],
            compiler_params=params(8),
            cost_estimate=cost(EARLY_FLOPS, 10**6),
            name="early_slots",
        )(me, kept, last))
    cloud = pl.pallas_call(
        functools.partial(kernel_out, devices, capacity, groups, field_count, early),
        in_specs=[in_vmem] + [in_hbm] * len(begun),
        out_specs=in_hbm,
        out_shape=out_shape,
        input_output_aliases={1: 0} if begun else {},
        scratch_shapes=[
            pltpu.VMEM(((block_count - early) * owned, slots), f32),
            pltpu.SemaphoreType.DMA((block_count - early,)),
        ],
        compiler_params=params(16),
        name="cloud_slots",
    )(received.reshape(-1, owned), *begun)
    return cloud.reshape(field_count, levels, width, slots), gcm_out


def solution(mesh):
    return jax.shard_map(
        body,
        mesh=mesh,
        in_specs=(
            P(None, None, None, ("ex", "ey")),
            P(None, None, "ex", "ey", None, None),
            P(None, "ex", "ey", None, None),
            P(("ex", "ey"), None),
            P(("ex", "ey")),
        ),
        out_specs=(P(None, None, None, ("ex", "ey")), P(None, None, "ex", "ey", None, None)),
        check_vma=False,
    )
```

```python
import functools

import jax
import jax.numpy as jnp
from jax import lax
from jax.experimental import pallas as pl
from jax.experimental.pallas import tpu as pltpu
from jax.sharding import PartitionSpec as P

diffusion = 0.1
advection = 0.15
buoyancy = 0.3
latent_heat = 0.5
fallout = 0.2
condense_rate = 0.4
nudging = 0.5

AXES = ("ex", "ey")
NT = (((1,), (1,)), ((), ()))
MIB = 1024 * 1024
REGROUP_FLOPS = 6*10**9
EARLY_BLOCKS = 3
EARLY_FLOPS = 13*10**9


def substep_level(values_at, nudge_row, z, levels, field_count, active=None):
    values = [values_at(f, z) for f in range(field_count)]
    width = values[0].shape[0]
    drift = (advection * 0.5) * values[0]
    from_east, from_west = diffusion - drift, diffusion + drift
    condensed = condense_rate * jnp.maximum(values[3], 0.0)
    results = []
    for f in range(field_count):
        v = values[f]
        east = pltpu.roll(v, width - 1, 0)
        west = pltpu.roll(v, 1, 0)
        fresh = east * from_east + west * from_west
        if 0 < z < levels - 1:
            fresh = fresh + diffusion * (values_at(f, z + 1) + values_at(f, z - 1))
        else:
            fresh = fresh + diffusion * values_at(f, z + 1 if z == 0 else z - 1)
        fresh = fresh + (nudge_row(f, z) - (nudging / width) * jnp.sum(v, axis=0, keepdims=True))
        own = 1.0 - 4.0 * diffusion
        if f == 1:
            fresh = fresh + buoyancy * values[2]
        elif f == 2:
            fresh = fresh - buoyancy * values[1] + latent_heat * condensed
        elif f == 3:
            fresh = fresh - condensed
        elif f == 4:
            fresh = fresh + condensed
            own = own - fallout
        fresh = fresh + own * v
        results.append(fresh if active is None else jnp.where(active, fresh, v))
    return results


def slot_rank(dest):
    owned = dest.shape[1]
    named = jnp.broadcast_to(dest.astype(jnp.float32), (owned, owned))
    rows = lax.broadcasted_iota(jnp.int32, (owned, owned), 0)
    cols = lax.broadcasted_iota(jnp.int32, (owned, owned), 1)
    earlier = jnp.where((named == named.T) & (rows < cols), 1, 0)
    return jnp.sum(earlier, axis=0, keepdims=True)


def one_hot_rows(slot, count):
    rows = lax.broadcasted_iota(jnp.int32, (count, slot.shape[1]), 0)
    return jnp.concatenate([jnp.where(rows == slot, 1.0, 0.0).astype(jnp.bfloat16)] * 3, axis=1)


def hop_bits(devices):
    bits = devices.bit_length() - 1
    return [bits - 1] + list(range(bits - 1))


def hop_order(difference, devices):
    place = jnp.zeros_like(difference)
    for bit in hop_bits(devices):
        place = 2 * place + ((difference >> bit) & 1)
    return place


def picked(picks, block):
    high = block.astype(jnp.bfloat16)
    rest = block - high.astype(jnp.float32)
    middle = rest.astype(jnp.bfloat16)
    low = (rest - middle.astype(jnp.float32)).astype(jnp.bfloat16)
    parts = jnp.concatenate([high, middle, low], axis=1)
    return lax.dot_general(picks, parts, NT, preferred_element_type=jnp.float32)


def fetch(source, target, sem):
    copy = pltpu.make_async_copy(source, target, sem)
    copy.start()
    return copy


def cloud_kernel(devices, capacity, early, me_ref, crm_hbm, gcm_hbm, mass_hbm, dest_hbm, cost_hbm,
                 send_hbm, far_hbm, near_hbm, nodes_ref, low_ref, high_ref, first_ref, second_ref, prof_ref, tend_ref,
                 crm_ref, gcm_ref, mass_ref, dest_ref, cost_ref, send_ref, early_ref, small_sem, crm_sem, send_sem, early_sem):
    field_count, levels, width, owned = crm_ref.shape
    group = owned // width
    small = [
        fetch(dest_hbm, dest_ref, small_sem.at[0]),
        fetch(gcm_hbm, gcm_ref, small_sem.at[1]),
        fetch(cost_hbm, cost_ref, small_sem.at[2]),
    ]
    pieces = [
        fetch(crm_hbm.at[:, pl.ds(z, group)], crm_ref.at[:, pl.ds(z, group)], crm_sem.at[z // group])
        for z in range(0, levels, group)
    ]
    small.append(fetch(mass_hbm, mass_ref, small_sem.at[3]))
    used = field_count * levels
    nodes = gcm_ref.shape[1]

    small[0].wait()
    rank = slot_rank(dest_ref[...])
    picks = one_hot_rows(dest_ref[...] * capacity + rank, devices * capacity)
    if early:
        turned = hop_order(dest_ref[...] ^ me_ref[0], devices)
        early_picks = one_hot_rows(turned * capacity + rank, devices * capacity)
    small[1].wait()
    grid_fields = jnp.concatenate(
        [gcm_ref[f] for f in range(field_count)] + [jnp.zeros((nodes, nodes - used), jnp.float32)], axis=1
    )
    prof_ref[...] = nudging * grid_fields.T
    small[2].wait()
    twice = jnp.broadcast_to(cost_ref[...] >= 2, (width, owned))

    def nudge_row(f, z):
        return prof_ref[pl.ds(f * levels + z, 1), :]

    def first_substep(z):
        fresh = substep_level(lambda f, k: crm_ref[f, k], nudge_row, z, levels, field_count)
        for f in range(field_count):
            first_ref[f, z] = fresh[f]

    def second_substep(z):
        fresh = substep_level(lambda f, k: first_ref[f, k], nudge_row, z, levels, field_count, twice)
        for f in range(field_count):
            second_ref[f, z] = fresh[f]

    pieces[0].wait()
    for z in range(levels):
        if (z + 1) % group == 0 and z + 1 < levels:
            pieces[(z + 1) // group].wait()
        first_substep(z)
    for z in range(levels):
        second_substep(z)

    sends = []
    if early:
        first = levels // group - 1
        at = field_count - early
        block = second_ref[pl.ds(at, early), pl.ds(first * group, group)].reshape(early * group * width, owned)
        moved = picked(early_picks, block)
        for e in range(early):
            rows = moved[:, e * owned:(e + 1) * owned].reshape(devices, capacity, owned)
            early_ref[:, e * capacity:(e + 1) * capacity, :] = rows
        half = devices // 2
        sends.append(fetch(early_ref.at[pl.ds(half, half)], far_hbm, early_sem.at[0]))
        sends.append(fetch(early_ref.at[pl.ds(0, half)], near_hbm, early_sem.at[1]))
    group_rows = field_count * capacity
    aligned = group_rows % 8 == 0
    for number in range(levels // group):
        held = field_count - (early if number == levels // group - 1 else 0)
        blocks = second_ref[pl.ds(0, held), pl.ds(number * group, group)].reshape(held * group * width, owned)
        moved = picked(picks, blocks)
        for f in range(held):
            at = (number * field_count + f) * capacity
            send_ref[:, at:at + capacity, :] = moved[:, f * owned:(f + 1) * owned].reshape(devices, capacity, owned)
        if aligned:
            part = pl.ds(number * group_rows, held * capacity)
            sends.append(fetch(send_ref.at[:, part], send_hbm.at[:, part], send_sem.at[number]))
    if not aligned:
        sends.append(fetch(send_ref, send_hbm, send_sem.at[0]))

    tend_ref[...] = jnp.zeros_like(tend_ref)
    for f in range(field_count):
        for z in range(levels):
            gained = jnp.sum(second_ref[f, z] - crm_ref[f, z], axis=0, keepdims=True) * (1.0 / width)
            tend_ref[pl.ds(f * levels + z, 1), :] = gained
    small[3].wait()
    mass = mass_ref[...]
    fields = jnp.concatenate(
        [gcm_ref[f] for f in range(field_count)] + [mass, jnp.zeros((nodes, nodes - used - levels), jnp.float32)],
        axis=1,
    )
    factors = jnp.concatenate([mass] * field_count + [jnp.ones((nodes, nodes - used), jnp.float32)], axis=1)
    nodes_ref[...] = (fields + tend_ref[...].T) * factors
    return sends


def edges_y(elx, ely, side, nodes_ref, low_ref, high_ref):
    step = side * side
    for a in range(elx):
        first = a * ely * step
        final = (a * ely + ely - 1) * step + side - 1
        low_ref[a * side:(a + 1) * side, :] = nodes_ref[pl.ds(first, side, stride=side), :]
        high_ref[a * side:(a + 1) * side, :] = nodes_ref[pl.ds(final, side, stride=side), :]


def kernel_a(devices, capacity, early, elx, ely, side, *refs):
    sends = cloud_kernel(devices, capacity, early, *refs)
    edges_y(elx, ely, side, *refs[9:12])
    for copy in sends:
        copy.wait()


def kernel_y(elx, ely, side, nodes_ref, south_ref, north_ref, sum_ref, low_ref, high_ref):
    step = side * side
    sum_ref[...] = nodes_ref[...]
    for a in range(elx):
        for b in range(ely):
            base = (a * ely + b) * step
            if b > 0:
                gain = nodes_ref[pl.ds(base - step + side - 1, side, stride=side), :]
            else:
                gain = south_ref[a * side:(a + 1) * side, :]
            here = pl.ds(base, side, stride=side)
            sum_ref[here, :] = nodes_ref[here, :] + gain
            if b + 1 < ely:
                gain = nodes_ref[pl.ds(base + step, side, stride=side), :]
            else:
                gain = north_ref[a * side:(a + 1) * side, :]
            here = pl.ds(base + side - 1, side, stride=side)
            sum_ref[here, :] = nodes_ref[here, :] + gain
    for b in range(ely):
        low_ref[b * side:(b + 1) * side, :] = sum_ref[b * step:b * step + side, :]
        start = (elx - 1) * ely * step + b * step + (side - 1) * side
        high_ref[b * side:(b + 1) * side, :] = sum_ref[start:start + side, :]


def sum_first(elx, ely, side, sum_ref, west_ref, east_ref, out_ref, full_ref):
    step = side * side
    field_count, nodes, levels = out_ref.shape
    full_ref[...] = sum_ref[...]
    for a in range(elx):
        for b in range(ely):
            base = (a * ely + b) * step
            last = base + (side - 1) * side
            if a > 0:
                before = ((a - 1) * ely + b) * step + (side - 1) * side
                gain = sum_ref[before:before + side, :]
            else:
                gain = west_ref[b * side:(b + 1) * side, :]
            full_ref[base:base + side, :] = sum_ref[base:base + side, :] + gain
            if a + 1 < elx:
                after = ((a + 1) * ely + b) * step
                gain = sum_ref[after:after + side, :]
            else:
                gain = east_ref[b * side:(b + 1) * side, :]
            full_ref[last:last + side, :] = sum_ref[last:last + side, :] + gain
    full = full_ref[...]
    divisor = full[:, field_count * levels:(field_count + 1) * levels]
    for f in range(field_count):
        out_ref[f] = full[:, f * levels:(f + 1) * levels] / divisor


def turned_blocks(rows_of, out_hbm, out_ref, sem):
    block = out_ref.shape[0] // len(rows_of)
    copies = []
    for number, (step, slots_at) in enumerate(rows_of):
        here, there = pl.ds(number * block, block), pl.ds(step * block, block)
        out_ref[here, :] = slots_at().T
        copies.append(fetch(out_ref.at[here], out_hbm.at[there], sem.at[number]))
    return copies


def kernel_out(devices, capacity, groups, field_count, early, sizes, recv_ref, sum_ref, west_ref, east_ref, *refs):
    out_hbm, gcm_hbm, out_ref, gcm_ref, full_ref, sem, gcm_sem = refs[-7:]
    sum_first(*sizes, sum_ref, west_ref, east_ref, gcm_ref, full_ref)
    gcm_copy = fetch(gcm_ref, gcm_hbm, gcm_sem)
    pitch = recv_ref.shape[0] // devices

    def rows(first):
        ranked = [recv_ref[pl.ds(first + r, devices, stride=pitch), :] for r in range(capacity)]
        return jnp.concatenate(ranked, axis=0)

    blocks = groups * field_count - early
    steps = [(at % field_count) * groups + at // field_count for at in range(blocks)]
    rows_of = [(step, functools.partial(rows, at * capacity)) for at, step in enumerate(steps)]
    for copy in [gcm_copy] + turned_blocks(rows_of, out_hbm, out_ref, sem):
        copy.wait()


def kernel_early(devices, capacity, groups, field_count, early, sources, me_ref, *refs):
    slots = devices * capacity
    *blocks, out_hbm, row_ref, out_ref, sem = refs
    arrived = [(ref, index) for ref in blocks for index in range(ref.shape[0])]
    for (ref, index), bits in zip(arrived, sources):
        for e in range(early):
            tile = ref[index, pl.ds(e * capacity, capacity), :]
            row_ref[pl.ds(e * slots + (me_ref[0] ^ bits), capacity, stride=devices), :] = tile
    steps = [(field_count - early + e) * groups + groups - 1 for e in range(early)]
    rows_of = [(step, lambda e=e: row_ref[e * slots:(e + 1) * slots, :]) for e, step in enumerate(steps)]
    for copy in turned_blocks(rows_of, out_hbm, out_ref, sem):
        copy.wait()


def params(mib):
    return pltpu.CompilerParams(vmem_limit_bytes=mib * MIB)


def cost(flops, byte_count):
    return pl.CostEstimate(flops=flops, bytes_accessed=byte_count, transcendentals=0)


def shift(face, axis, by):
    count = lax.axis_size(axis)
    return lax.ppermute(face, axis, [(i, (i + by) % count) for i in range(count)])


def exchange(block, bits):
    count = lax.axis_size(AXES)
    return lax.ppermute(block, AXES, [(i, i ^ bits) for i in range(count)])


def kernel_regroup(kept_ref, last_ref, *out_refs):
    count = kept_ref.shape[1] // len(out_refs)
    for number, out_ref in enumerate(out_refs):
        part = pl.ds(number * count, count)
        out_ref[0:1] = kept_ref[:, part]
        out_ref[1:2] = last_ref[:, part]


def regrouped(arrays, ways, first):
    count = arrays[0].shape[1] // ways
    if first:
        shape = jax.ShapeDtypeStruct((2, count) + arrays[0].shape[2:], arrays[0].dtype)
        return pl.pallas_call(
            kernel_regroup,
            out_shape=[shape] * ways,
            compiler_params=params(8),
            cost_estimate=cost(REGROUP_FLOPS, 10**6),
            name="regroup",
        )(*arrays)
    return [jnp.concatenate([a[:, i * count:(i + 1) * count] for a in arrays]) for i in range(ways)]


def hops(near, far, devices):
    top, *others = hop_bits(devices)
    arrays = [near[None], exchange(far, 1 << top)[None]]
    senders = [0, 1 << top]
    middle = len(others) - 1
    steps = [others[:1], others[1:middle], others[middle:]]
    for step in steps:
        moves = [0]
        for bit in step:
            moves = [move | flip for move in moves for flip in (0, 1 << bit)]
        parts = regrouped(arrays, len(moves), step is steps[0])
        arrays = [exchange(part, move) if move else part for part, move in zip(parts, moves)]
        senders = [sender ^ move for move in moves for sender in senders]
    return [array[:, 0] for array in arrays], senders


def body(crm_state, gcm_state, mass, dest, cost_class):
    devices = lax.axis_size(("ex", "ey"))
    field_count, levels, width, owned = crm_state.shape
    elx, ely, side = gcm_state.shape[2:5]
    capacity = max(2, 2 * owned // devices)
    slots = capacity * devices
    values = field_count * levels * width
    f32 = jnp.float32
    gcm_nodes = gcm_state.transpose(0, 2, 3, 4, 5, 1).reshape(field_count, owned, levels)
    mass_nodes = mass.transpose(1, 2, 3, 4, 0).reshape(owned, levels)
    sizes = (elx, ely, side)
    face_x = jax.ShapeDtypeStruct((ely * side, owned), f32)
    face_y = jax.ShapeDtypeStruct((elx * side, owned), f32)
    in_hbm = pl.BlockSpec(memory_space=pltpu.HBM)
    in_vmem = pl.BlockSpec(memory_space=pltpu.VMEM)
    square = jax.ShapeDtypeStruct((owned, owned), f32)
    in_smem = pl.BlockSpec(memory_space=pltpu.SMEM)
    me = lax.axis_index(AXES).astype(jnp.int32).reshape(1)
    groups = levels * width // owned
    early = EARLY_BLOCKS if capacity % 8 == 0 and devices & (devices - 1) == 0 else 0
    packed = (devices, (values // owned - early) * capacity, owned)
    apart = (max(2, devices) // 2, max(1, early) * capacity, owned)
    send, far, near, nodes, low, high = pl.pallas_call(
        functools.partial(kernel_a, devices, capacity, early, *sizes),
        out_shape=(
            jax.ShapeDtypeStruct(packed, f32),
            jax.ShapeDtypeStruct(apart, f32),
            jax.ShapeDtypeStruct(apart, f32),
            square,
            face_y,
            face_y,
        ),
        in_specs=[in_smem] + [in_hbm] * 5,
        out_specs=(in_hbm, in_hbm, in_hbm, in_vmem, in_vmem, in_vmem),
        scratch_shapes=[
            pltpu.VMEM(crm_state.shape, f32),
            pltpu.VMEM(crm_state.shape, f32),
            pltpu.VMEM((owned, owned), f32),
            pltpu.VMEM((owned, owned), f32),
            pltpu.VMEM(crm_state.shape, f32),
            pltpu.VMEM(gcm_nodes.shape, f32),
            pltpu.VMEM(mass_nodes.shape, f32),
            pltpu.VMEM((1, owned), jnp.int32),
            pltpu.VMEM((1, owned), jnp.int32),
            pltpu.VMEM(packed, f32),
            pltpu.VMEM((devices,) + apart[1:], f32),
            pltpu.SemaphoreType.DMA((4,)),
            pltpu.SemaphoreType.DMA((groups,)),
            pltpu.SemaphoreType.DMA((groups,)),
            pltpu.SemaphoreType.DMA((2,)),
        ],
        compiler_params=params(63),
        name="cloud_models",
    )(me, crm_state, gcm_nodes, mass_nodes, dest.reshape(1, owned), cost_class.reshape(1, owned))
    received = lax.all_to_all(send, AXES, split_axis=0, concat_axis=0, tiled=True)
    if early:
        arrived, sources = hops(near, far, devices)
    north = shift(low, "ey", -1)
    south = shift(high, "ey", 1)
    summed, low, high = pl.pallas_call(
        functools.partial(kernel_y, *sizes),
        out_shape=(square, face_x, face_x),
        compiler_params=params(8),
        cost_estimate=cost(10**5, 10**5),
        name="edge_sum_second",
    )(nodes, south, north)
    east = shift(low, "ex", -1)
    west = shift(high, "ex", 1)
    if early:
        summed, arrived[-1] = lax.optimization_barrier((summed, arrived[-1]))
    out_shape = jax.ShapeDtypeStruct((values, slots), f32)
    block_count = values // owned
    begun = []
    if early:
        begun.append(pl.pallas_call(
            functools.partial(kernel_early, devices, capacity, groups, field_count, early, sources),
            in_specs=[in_smem] + [in_vmem] * len(arrived),
            out_specs=in_hbm,
            out_shape=out_shape,
            scratch_shapes=[
                pltpu.VMEM((early * slots, owned), f32),
                pltpu.VMEM((early * owned, slots), f32),
                pltpu.SemaphoreType.DMA((early,)),
            ],
            compiler_params=params(8),
            cost_estimate=cost(EARLY_FLOPS, 10**6),
            name="early_slots",
        )(me, *arrived))
    cloud, gcm_out = pl.pallas_call(
        functools.partial(kernel_out, devices, capacity, groups, field_count, early, sizes),
        in_specs=[in_vmem] * 4 + [in_hbm] * len(begun),
        out_specs=(in_hbm, in_hbm),
        out_shape=(out_shape, jax.ShapeDtypeStruct((field_count, owned, levels), f32)),
        input_output_aliases={4: 0} if begun else {},
        scratch_shapes=[
            pltpu.VMEM(((block_count - early) * owned, slots), f32),
            pltpu.VMEM((field_count, owned, levels), f32),
            pltpu.VMEM((owned, owned), f32),
            pltpu.SemaphoreType.DMA((block_count - early,)),
            pltpu.SemaphoreType.DMA,
        ],
        compiler_params=params(16),
        name="cloud_slots",
    )(received.reshape(-1, owned), summed, west, east, *begun)
    gcm_out = gcm_out.reshape(field_count, elx, ely, side, side, levels).transpose(0, 5, 1, 2, 3, 4)
    return cloud.reshape(field_count, levels, width, slots), gcm_out


def solution(mesh):
    return jax.shard_map(
        body,
        mesh=mesh,
        in_specs=(
            P(None, None, None, ("ex", "ey")),
            P(None, None, "ex", "ey", None, None),
            P(None, "ex", "ey", None, None),
            P(("ex", "ey"), None),
            P(("ex", "ey")),
        ),
        out_specs=(P(None, None, None, ("ex", "ey")), P(None, None, "ex", "ey", None, None)),
        check_vma=False,
    )
```

```python
import functools

import jax
import jax.numpy as jnp
from jax import lax
from jax.experimental import pallas as pl
from jax.experimental.pallas import tpu as pltpu
from jax.sharding import PartitionSpec as P

diffusion = 0.1
advection = 0.15
buoyancy = 0.3
latent_heat = 0.5
fallout = 0.2
condense_rate = 0.4
nudging = 0.5

AXES = ("ex", "ey")
NT = (((1,), (1,)), ((), ()))
MIB = 1024 * 1024
REGROUP_FLOPS = 6*10**9
EARLY_BLOCKS = 3
EARLY_FLOPS = 13*10**9


def substep_level(values_at, nudge_row, z, levels, field_count, active=None):
    values = [values_at(f, z) for f in range(field_count)]
    width = values[0].shape[0]
    drift = (advection * 0.5) * values[0]
    from_east, from_west = diffusion - drift, diffusion + drift
    condensed = condense_rate * jnp.maximum(values[3], 0.0)
    results = []
    for f in range(field_count):
        v = values[f]
        east = pltpu.roll(v, width - 1, 0)
        west = pltpu.roll(v, 1, 0)
        fresh = east * from_east + west * from_west
        if 0 < z < levels - 1:
            fresh = fresh + diffusion * (values_at(f, z + 1) + values_at(f, z - 1))
        else:
            fresh = fresh + diffusion * values_at(f, z + 1 if z == 0 else z - 1)
        fresh = fresh + (nudge_row(f, z) - (nudging / width) * jnp.sum(v, axis=0, keepdims=True))
        own = 1.0 - 4.0 * diffusion
        if f == 1:
            fresh = fresh + buoyancy * values[2]
        elif f == 2:
            fresh = fresh - buoyancy * values[1] + latent_heat * condensed
        elif f == 3:
            fresh = fresh - condensed
        elif f == 4:
            fresh = fresh + condensed
            own = own - fallout
        fresh = fresh + own * v
        results.append(fresh if active is None else jnp.where(active, fresh, v))
    return results


def slot_rank(dest):
    owned = dest.shape[1]
    named = jnp.broadcast_to(dest.astype(jnp.float32), (owned, owned))
    rows = lax.broadcasted_iota(jnp.int32, (owned, owned), 0)
    cols = lax.broadcasted_iota(jnp.int32, (owned, owned), 1)
    earlier = jnp.where((named == named.T) & (rows < cols), 1, 0)
    return jnp.sum(earlier, axis=0, keepdims=True)


def one_hot_rows(slot, count):
    rows = lax.broadcasted_iota(jnp.int32, (count, slot.shape[1]), 0)
    return jnp.concatenate([jnp.where(rows == slot, 1.0, 0.0).astype(jnp.bfloat16)] * 3, axis=1)


def hop_bits(devices):
    bits = devices.bit_length() - 1
    return [bits - 1] + list(range(bits - 1))


def hop_order(difference, devices):
    place = jnp.zeros_like(difference)
    for bit in hop_bits(devices):
        place = 2 * place + ((difference >> bit) & 1)
    return place


def picked(picks, block):
    high = block.astype(jnp.bfloat16)
    rest = block - high.astype(jnp.float32)
    middle = rest.astype(jnp.bfloat16)
    low = (rest - middle.astype(jnp.float32)).astype(jnp.bfloat16)
    parts = jnp.concatenate([high, middle, low], axis=1)
    return lax.dot_general(picks, parts, NT, preferred_element_type=jnp.float32)


def fetch(source, target, sem):
    copy = pltpu.make_async_copy(source, target, sem)
    copy.start()
    return copy


def cloud_kernel(devices, capacity, early, me_ref, crm_hbm, gcm_hbm, mass_hbm, dest_hbm, cost_hbm,
                 send_hbm, far_hbm, near_hbm, nodes_ref, low_ref, high_ref, first_ref, second_ref, prof_ref, tend_ref,
                 crm_ref, gcm_ref, mass_ref, dest_ref, cost_ref, send_ref, early_ref, small_sem, crm_sem, send_sem, early_sem):
    field_count, levels, width, owned = crm_ref.shape
    group = owned // width
    small = [
        fetch(dest_hbm, dest_ref, small_sem.at[0]),
        fetch(gcm_hbm, gcm_ref, small_sem.at[1]),
        fetch(cost_hbm, cost_ref, small_sem.at[2]),
    ]
    pieces = [
        fetch(crm_hbm.at[:, pl.ds(z, group)], crm_ref.at[:, pl.ds(z, group)], crm_sem.at[z // group])
        for z in range(0, levels, group)
    ]
    small.append(fetch(mass_hbm, mass_ref, small_sem.at[3]))
    used = field_count * levels
    nodes = gcm_ref.shape[1]

    small[0].wait()
    rank = slot_rank(dest_ref[...])
    picks = one_hot_rows(dest_ref[...] * capacity + rank, devices * capacity)
    if early:
        turned = hop_order(dest_ref[...] ^ me_ref[0], devices)
        early_picks = one_hot_rows(turned * capacity + rank, devices * capacity)
    small[1].wait()
    grid_fields = jnp.concatenate(
        [gcm_ref[f] for f in range(field_count)] + [jnp.zeros((nodes, nodes - used), jnp.float32)], axis=1
    )
    prof_ref[...] = nudging * grid_fields.T
    small[2].wait()
    twice = jnp.broadcast_to(cost_ref[...] >= 2, (width, owned))

    def nudge_row(f, z):
        return prof_ref[pl.ds(f * levels + z, 1), :]

    def first_substep(z):
        fresh = substep_level(lambda f, k: crm_ref[f, k], nudge_row, z, levels, field_count)
        for f in range(field_count):
            first_ref[f, z] = fresh[f]

    def second_substep(z):
        fresh = substep_level(lambda f, k: first_ref[f, k], nudge_row, z, levels, field_count, twice)
        for f in range(field_count):
            second_ref[f, z] = fresh[f]

    pieces[0].wait()
    for z in range(levels):
        if (z + 1) % group == 0 and z + 1 < levels:
            pieces[(z + 1) // group].wait()
        first_substep(z)
    for z in range(levels):
        second_substep(z)

    sends = []
    if early:
        first = levels // group - 1
        at = field_count - early
        block = second_ref[pl.ds(at, early), pl.ds(first * group, group)].reshape(early * group * width, owned)
        moved = picked(early_picks, block)
        for e in range(early):
            rows = moved[:, e * owned:(e + 1) * owned].reshape(devices, capacity, owned)
            early_ref[:, e * capacity:(e + 1) * capacity, :] = rows
        half = devices // 2
        sends.append(fetch(early_ref.at[pl.ds(half, half)], far_hbm, early_sem.at[0]))
        sends.append(fetch(early_ref.at[pl.ds(0, half)], near_hbm, early_sem.at[1]))
    group_rows = field_count * capacity
    aligned = group_rows % 8 == 0
    for number in range(levels // group):
        held = field_count - (early if number == levels // group - 1 else 0)
        blocks = second_ref[pl.ds(0, held), pl.ds(number * group, group)].reshape(held * group * width, owned)
        moved = picked(picks, blocks)
        for f in range(held):
            at = (number * field_count + f) * capacity
            send_ref[:, at:at + capacity, :] = moved[:, f * owned:(f + 1) * owned].reshape(devices, capacity, owned)
        if aligned:
            part = pl.ds(number * group_rows, held * capacity)
            sends.append(fetch(send_ref.at[:, part], send_hbm.at[:, part], send_sem.at[number]))
    if not aligned:
        sends.append(fetch(send_ref, send_hbm, send_sem.at[0]))

    tend_ref[...] = jnp.zeros_like(tend_ref)
    for f in range(field_count):
        for z in range(levels):
            gained = jnp.sum(second_ref[f, z] - crm_ref[f, z], axis=0, keepdims=True) * (1.0 / width)
            tend_ref[pl.ds(f * levels + z, 1), :] = gained
    small[3].wait()
    mass = mass_ref[...]
    fields = jnp.concatenate(
        [gcm_ref[f] for f in range(field_count)] + [mass, jnp.zeros((nodes, nodes - used - levels), jnp.float32)],
        axis=1,
    )
    factors = jnp.concatenate([mass] * field_count + [jnp.ones((nodes, nodes - used), jnp.float32)], axis=1)
    nodes_ref[...] = (fields + tend_ref[...].T) * factors
    return sends


def edges_y(elx, ely, side, nodes_ref, low_ref, high_ref):
    step = side * side
    for a in range(elx):
        first = a * ely * step
        final = (a * ely + ely - 1) * step + side - 1
        low_ref[a * side:(a + 1) * side, :] = nodes_ref[pl.ds(first, side, stride=side), :]
        high_ref[a * side:(a + 1) * side, :] = nodes_ref[pl.ds(final, side, stride=side), :]


def kernel_a(devices, capacity, early, elx, ely, side, *refs):
    sends = cloud_kernel(devices, capacity, early, *refs)
    edges_y(elx, ely, side, *refs[9:12])
    for copy in sends:
        copy.wait()


def divided(rows, levels, field, fields):
    mass = rows[:, fields * levels:(fields + 1) * levels]
    return rows[:, field * levels:(field + 1) * levels] / mass


def face_rows(elx, ely, side):
    step = side * side
    low = [b * step for b in range(ely)]
    return low, [((elx - 1) * ely + b) * step + (side - 1) * side for b in range(ely)]


def kernel_y(elx, ely, side, nodes_ref, south_ref, north_ref, part_ref, low_ref, high_ref, sum_ref, full_ref):
    step = side * side
    field_count, _, levels = part_ref.shape
    sum_ref[...] = nodes_ref[...]
    for a in range(elx):
        for b in range(ely):
            base = (a * ely + b) * step
            if b > 0:
                gain = nodes_ref[pl.ds(base - step + side - 1, side, stride=side), :]
            else:
                gain = south_ref[a * side:(a + 1) * side, :]
            here = pl.ds(base, side, stride=side)
            sum_ref[here, :] = nodes_ref[here, :] + gain
            if b + 1 < ely:
                gain = nodes_ref[pl.ds(base + step, side, stride=side), :]
            else:
                gain = north_ref[a * side:(a + 1) * side, :]
            here = pl.ds(base + side - 1, side, stride=side)
            sum_ref[here, :] = nodes_ref[here, :] + gain
    for face_ref, starts in zip((low_ref, high_ref), face_rows(elx, ely, side)):
        for b, start in enumerate(starts):
            face_ref[b * side:(b + 1) * side, :] = sum_ref[start:start + side, :]
    full_ref[...] = sum_ref[...]
    for a in range(elx - 1):
        for b in range(ely):
            last = (a * ely + b) * step + (side - 1) * side
            after = ((a + 1) * ely + b) * step
            joined = sum_ref[last:last + side, :] + sum_ref[after:after + side, :]
            full_ref[last:last + side, :] = joined
            full_ref[after:after + side, :] = joined
    full = full_ref[...]
    for f in range(field_count):
        part_ref[f] = divided(full, levels, f, field_count)


def complete_faces(elx, ely, side, low_ref, high_ref, west_ref, east_ref, gcm_ref):
    field_count, _, levels = gcm_ref.shape
    lows, highs = face_rows(elx, ely, side)
    for own_ref, sent_ref, starts in ((low_ref, west_ref, lows), (high_ref, east_ref, highs)):
        rows = own_ref[...] + sent_ref[...]
        for f in range(field_count):
            quotient = divided(rows, levels, f, field_count)
            for b, start in enumerate(starts):
                gcm_ref[f, start:start + side, :] = quotient[b * side:(b + 1) * side]


def turned_blocks(rows_of, out_hbm, out_ref, sem):
    block = out_ref.shape[0] // len(rows_of)
    copies = []
    for number, (step, slots_at) in enumerate(rows_of):
        here, there = pl.ds(number * block, block), pl.ds(step * block, block)
        out_ref[here, :] = slots_at().T
        copies.append(fetch(out_ref.at[here], out_hbm.at[there], sem.at[number]))
    return copies


def kernel_out(devices, capacity, groups, field_count, early, sizes, recv_ref, part_ref, west_ref, east_ref,
               low_ref, high_ref, *refs):
    out_hbm, gcm_hbm, out_ref, gcm_ref, spread_ref, sem, gcm_sem = refs[-7:]
    gcm_ref[...] = part_ref[...]
    complete_faces(*sizes, low_ref, high_ref, west_ref, east_ref, gcm_ref)
    gcm_copy = fetch(gcm_ref, gcm_hbm, gcm_sem)
    pitch = recv_ref.shape[0] // devices

    rows_ref = recv_ref
    if pitch % 16 == 0:
        rows_ref = spread_ref
        for source in range(devices):
            spread_ref[pl.ds(source * (pitch + 8), pitch), :] = recv_ref[pl.ds(source * pitch, pitch), :]
        pitch = pitch + 8

    def rows(first):
        ranked = [rows_ref[pl.ds(first + r, devices, stride=pitch), :] for r in range(capacity)]
        return jnp.concatenate(ranked, axis=0)

    blocks = groups * field_count - early
    steps = [(at % field_count) * groups + at // field_count for at in range(blocks)]
    rows_of = [(step, functools.partial(rows, at * capacity)) for at, step in enumerate(steps)]
    for copy in [gcm_copy] + turned_blocks(rows_of, out_hbm, out_ref, sem):
        copy.wait()


def kernel_early(devices, capacity, groups, field_count, early, sources, me_ref, *refs):
    apart = devices + 8
    slots = apart * capacity
    *blocks, out_hbm, row_ref, out_ref, sem = refs
    arrived = [(ref, index) for ref in blocks for index in range(ref.shape[0])]
    for (ref, index), bits in zip(arrived, sources):
        for e in range(early):
            tile = ref[index, pl.ds(e * capacity, capacity), :]
            row_ref[pl.ds(e * slots + (me_ref[0] ^ bits), capacity, stride=apart), :] = tile
    steps = [(field_count - early + e) * groups + groups - 1 for e in range(early)]

    def slots_at(first):
        ranked = [row_ref[first + r * apart:first + r * apart + devices, :] for r in range(capacity)]
        return jnp.concatenate(ranked, axis=0)

    rows_of = [(step, functools.partial(slots_at, e * slots)) for e, step in enumerate(steps)]
    for copy in turned_blocks(rows_of, out_hbm, out_ref, sem):
        copy.wait()


def params(mib):
    return pltpu.CompilerParams(vmem_limit_bytes=mib * MIB)


def cost(flops, byte_count):
    return pl.CostEstimate(flops=flops, bytes_accessed=byte_count, transcendentals=0)


def shift(face, axis, by):
    count = lax.axis_size(axis)
    return lax.ppermute(face, axis, [(i, (i + by) % count) for i in range(count)])


def exchange(block, bits):
    count = lax.axis_size(AXES)
    return lax.ppermute(block, AXES, [(i, i ^ bits) for i in range(count)])


def kernel_regroup(kept_ref, last_ref, *out_refs):
    count = kept_ref.shape[1] // len(out_refs)
    for number, out_ref in enumerate(out_refs):
        part = pl.ds(number * count, count)
        out_ref[0:1] = kept_ref[:, part]
        out_ref[1:2] = last_ref[:, part]


def regrouped(arrays, ways, first):
    count = arrays[0].shape[1] // ways
    if first:
        shape = jax.ShapeDtypeStruct((2, count) + arrays[0].shape[2:], arrays[0].dtype)
        return pl.pallas_call(
            kernel_regroup,
            out_shape=[shape] * ways,
            compiler_params=params(8),
            cost_estimate=cost(REGROUP_FLOPS, 10**6),
            name="regroup",
        )(*arrays)
    return [jnp.concatenate([a[:, i * count:(i + 1) * count] for a in arrays]) for i in range(ways)]


def hops(near, far, devices):
    top, *others = hop_bits(devices)
    arrays = [near[None], exchange(far, 1 << top)[None]]
    senders = [0, 1 << top]
    middle = len(others) - 1
    steps = [others[:1], others[1:middle], others[middle:]]
    for step in steps:
        moves = [0]
        for bit in step:
            moves = [move | flip for move in moves for flip in (0, 1 << bit)]
        parts = regrouped(arrays, len(moves), step is steps[0])
        arrays = [exchange(part, move) if move else part for part, move in zip(parts, moves)]
        senders = [sender ^ move for move in moves for sender in senders]
    return [array[:, 0] for array in arrays], senders


def body(crm_state, gcm_state, mass, dest, cost_class):
    devices = lax.axis_size(("ex", "ey"))
    field_count, levels, width, owned = crm_state.shape
    elx, ely, side = gcm_state.shape[2:5]
    capacity = max(2, 2 * owned // devices)
    slots = capacity * devices
    values = field_count * levels * width
    f32 = jnp.float32
    gcm_nodes = gcm_state.transpose(0, 2, 3, 4, 5, 1).reshape(field_count, owned, levels)
    mass_nodes = mass.transpose(1, 2, 3, 4, 0).reshape(owned, levels)
    sizes = (elx, ely, side)
    face_x = jax.ShapeDtypeStruct((ely * side, owned), f32)
    face_y = jax.ShapeDtypeStruct((elx * side, owned), f32)
    in_hbm = pl.BlockSpec(memory_space=pltpu.HBM)
    in_vmem = pl.BlockSpec(memory_space=pltpu.VMEM)
    square = jax.ShapeDtypeStruct((owned, owned), f32)
    in_smem = pl.BlockSpec(memory_space=pltpu.SMEM)
    me = lax.axis_index(AXES).astype(jnp.int32).reshape(1)
    groups = levels * width // owned
    early = EARLY_BLOCKS if capacity % 8 == 0 and devices & (devices - 1) == 0 else 0
    packed = (devices, (values // owned - early) * capacity, owned)
    apart = (max(2, devices) // 2, max(1, early) * capacity, owned)
    send, far, near, nodes, low, high = pl.pallas_call(
        functools.partial(kernel_a, devices, capacity, early, *sizes),
        out_shape=(
            jax.ShapeDtypeStruct(packed, f32),
            jax.ShapeDtypeStruct(apart, f32),
            jax.ShapeDtypeStruct(apart, f32),
            square,
            face_y,
            face_y,
        ),
        in_specs=[in_smem] + [in_hbm] * 5,
        out_specs=(in_hbm, in_hbm, in_hbm, in_vmem, in_vmem, in_vmem),
        scratch_shapes=[
            pltpu.VMEM(crm_state.shape, f32),
            pltpu.VMEM(crm_state.shape, f32),
            pltpu.VMEM((owned, owned), f32),
            pltpu.VMEM((owned, owned), f32),
            pltpu.VMEM(crm_state.shape, f32),
            pltpu.VMEM(gcm_nodes.shape, f32),
            pltpu.VMEM(mass_nodes.shape, f32),
            pltpu.VMEM((1, owned), jnp.int32),
            pltpu.VMEM((1, owned), jnp.int32),
            pltpu.VMEM(packed, f32),
            pltpu.VMEM((devices,) + apart[1:], f32),
            pltpu.SemaphoreType.DMA((4,)),
            pltpu.SemaphoreType.DMA((groups,)),
            pltpu.SemaphoreType.DMA((groups,)),
            pltpu.SemaphoreType.DMA((2,)),
        ],
        compiler_params=params(63),
        name="cloud_models",
    )(me, crm_state, gcm_nodes, mass_nodes, dest.reshape(1, owned), cost_class.reshape(1, owned))
    received = lax.all_to_all(send, AXES, split_axis=0, concat_axis=0, tiled=True)
    if early:
        arrived, sources = hops(near, far, devices)
    north = shift(low, "ey", -1)
    south = shift(high, "ey", 1)
    part, low, high = pl.pallas_call(
        functools.partial(kernel_y, *sizes),
        out_shape=(jax.ShapeDtypeStruct((field_count, owned, levels), f32), face_x, face_x),
        scratch_shapes=[pltpu.VMEM((owned, owned), f32)] * 2,
        compiler_params=params(8),
        cost_estimate=cost(10**5, 10**5),
        name="edge_sum_second",
    )(nodes, south, north)
    east = shift(low, "ex", -1)
    west = shift(high, "ex", 1)
    if early:
        part, arrived[-1] = lax.optimization_barrier((part, arrived[-1]))
    out_shape = jax.ShapeDtypeStruct((values, slots), f32)
    block_count = values // owned
    begun = []
    if early:
        begun.append(pl.pallas_call(
            functools.partial(kernel_early, devices, capacity, groups, field_count, early, sources),
            in_specs=[in_smem] + [in_vmem] * len(arrived),
            out_specs=in_hbm,
            out_shape=out_shape,
            scratch_shapes=[
                pltpu.VMEM((early * (devices + 8) * capacity, owned), f32),
                pltpu.VMEM((early * owned, slots), f32),
                pltpu.SemaphoreType.DMA((early,)),
            ],
            compiler_params=params(8),
            cost_estimate=cost(EARLY_FLOPS, 10**6),
            name="early_slots",
        )(me, *arrived))
    cloud, gcm_out = pl.pallas_call(
        functools.partial(kernel_out, devices, capacity, groups, field_count, early, sizes),
        in_specs=[in_vmem] * 6 + [in_hbm] * len(begun),
        out_specs=(in_hbm, in_hbm),
        out_shape=(out_shape, jax.ShapeDtypeStruct((field_count, owned, levels), f32)),
        input_output_aliases={6: 0} if begun else {},
        scratch_shapes=[
            pltpu.VMEM(((block_count - early) * owned, slots), f32),
            pltpu.VMEM((field_count, owned, levels), f32),
            pltpu.VMEM((devices * ((block_count - early) * capacity + 8), owned), f32),
            pltpu.SemaphoreType.DMA((block_count - early,)),
            pltpu.SemaphoreType.DMA,
        ],
        compiler_params=params(16),
        name="cloud_slots",
    )(received.reshape(-1, owned), part, west, east, low, high, *begun)
    gcm_out = gcm_out.reshape(field_count, elx, ely, side, side, levels).transpose(0, 5, 1, 2, 3, 4)
    return cloud.reshape(field_count, levels, width, slots), gcm_out


def solution(mesh):
    return jax.shard_map(
        body,
        mesh=mesh,
        in_specs=(
            P(None, None, None, ("ex", "ey")),
            P(None, None, "ex", "ey", None, None),
            P(None, "ex", "ey", None, None),
            P(("ex", "ey"), None),
            P(("ex", "ey")),
        ),
        out_specs=(P(None, None, None, ("ex", "ey")), P(None, None, "ex", "ey", None, None)),
        check_vma=False,
    )
```

```python
import functools

import jax
import jax.numpy as jnp
from jax import lax
from jax.experimental import pallas as pl
from jax.experimental.pallas import tpu as pltpu
from jax.sharding import PartitionSpec as P

diffusion = 0.1
advection = 0.15
buoyancy = 0.3
latent_heat = 0.5
fallout = 0.2
condense_rate = 0.4
nudging = 0.5

AXES = ("ex", "ey")
NT = (((1,), (1,)), ((), ()))
MIB = 1024 * 1024
REGROUP_FLOPS = 6*10**9
EARLY_BLOCKS = 3
EARLY_FLOPS = 13*10**9


def substep_level(values_at, nudge_row, z, levels, field_count, active=None):
    values = [values_at(f, z) for f in range(field_count)]
    width = values[0].shape[0]
    drift = (advection * 0.5) * values[0]
    from_east, from_west = diffusion - drift, diffusion + drift
    condensed = condense_rate * jnp.maximum(values[3], 0.0)
    results = []
    for f in range(field_count):
        v = values[f]
        east = pltpu.roll(v, width - 1, 0)
        west = pltpu.roll(v, 1, 0)
        fresh = east * from_east + west * from_west
        if 0 < z < levels - 1:
            fresh = fresh + diffusion * (values_at(f, z + 1) + values_at(f, z - 1))
        else:
            fresh = fresh + diffusion * values_at(f, z + 1 if z == 0 else z - 1)
        fresh = fresh + (nudge_row(f, z) - (nudging / width) * jnp.sum(v, axis=0, keepdims=True))
        own = 1.0 - 4.0 * diffusion
        if f == 1:
            fresh = fresh + buoyancy * values[2]
        elif f == 2:
            fresh = fresh - buoyancy * values[1] + latent_heat * condensed
        elif f == 3:
            fresh = fresh - condensed
        elif f == 4:
            fresh = fresh + condensed
            own = own - fallout
        fresh = fresh + own * v
        results.append(fresh if active is None else jnp.where(active, fresh, v))
    return results


def slot_rank(dest):
    owned = dest.shape[1]
    named = jnp.broadcast_to(dest.astype(jnp.float32), (owned, owned))
    rows = lax.broadcasted_iota(jnp.int32, (owned, owned), 0)
    cols = lax.broadcasted_iota(jnp.int32, (owned, owned), 1)
    earlier = jnp.where((named == named.T) & (rows < cols), 1, 0)
    return jnp.sum(earlier, axis=0, keepdims=True)


def one_hot_rows(slot, count):
    rows = lax.broadcasted_iota(jnp.int32, (count, slot.shape[1]), 0)
    return jnp.concatenate([jnp.where(rows == slot, 1.0, 0.0).astype(jnp.bfloat16)] * 3, axis=1)


def hop_bits(devices):
    bits = devices.bit_length() - 1
    return [bits - 1] + list(range(bits - 1))


def hop_order(difference, devices):
    place = jnp.zeros_like(difference)
    for bit in hop_bits(devices):
        place = 2 * place + ((difference >> bit) & 1)
    return place


def picked(picks, block):
    high = block.astype(jnp.bfloat16)
    rest = block - high.astype(jnp.float32)
    middle = rest.astype(jnp.bfloat16)
    low = (rest - middle.astype(jnp.float32)).astype(jnp.bfloat16)
    parts = jnp.concatenate([high, middle, low], axis=1)
    return lax.dot_general(picks, parts, NT, preferred_element_type=jnp.float32)


def fetch(source, target, sem):
    copy = pltpu.make_async_copy(source, target, sem)
    copy.start()
    return copy


def cloud_kernel(devices, capacity, early, me_ref, crm_hbm, gcm_hbm, mass_hbm, dest_hbm, cost_hbm,
                 send_hbm, far_hbm, near_hbm, nodes_ref, low_ref, high_ref, first_ref, second_ref, prof_ref, tend_ref,
                 crm_ref, gcm_ref, mass_ref, dest_ref, cost_ref, send_ref, early_ref, small_sem, crm_sem, send_sem, early_sem):
    field_count, levels, width, owned = crm_ref.shape
    group = owned // width
    small = [
        fetch(dest_hbm, dest_ref, small_sem.at[0]),
        fetch(gcm_hbm, gcm_ref, small_sem.at[1]),
        fetch(cost_hbm, cost_ref, small_sem.at[2]),
    ]
    pieces = [
        fetch(crm_hbm.at[:, pl.ds(z, group)], crm_ref.at[:, pl.ds(z, group)], crm_sem.at[z // group])
        for z in range(0, levels, group)
    ]
    small.append(fetch(mass_hbm, mass_ref, small_sem.at[3]))
    used = field_count * levels
    nodes = gcm_ref.shape[1]

    small[0].wait()
    rank = slot_rank(dest_ref[...])
    picks = one_hot_rows(dest_ref[...] * capacity + rank, devices * capacity)
    if early:
        turned = hop_order(dest_ref[...] ^ me_ref[0], devices)
        early_picks = one_hot_rows(turned * capacity + rank, devices * capacity)
    small[1].wait()
    grid_fields = jnp.concatenate(
        [gcm_ref[f] for f in range(field_count)] + [jnp.zeros((nodes, nodes - used), jnp.float32)], axis=1
    )
    prof_ref[...] = nudging * grid_fields.T
    small[2].wait()
    twice = jnp.broadcast_to(cost_ref[...] >= 2, (width, owned))

    def nudge_row(f, z):
        return prof_ref[pl.ds(f * levels + z, 1), :]

    def first_substep(z):
        fresh = substep_level(lambda f, k: crm_ref[f, k], nudge_row, z, levels, field_count)
        for f in range(field_count):
            first_ref[f, z] = fresh[f]

    def second_substep(z):
        fresh = substep_level(lambda f, k: first_ref[f, k], nudge_row, z, levels, field_count, twice)
        for f in range(field_count):
            second_ref[f, z] = fresh[f]

    pieces[0].wait()
    for z in range(levels):
        if (z + 1) % group == 0 and z + 1 < levels:
            pieces[(z + 1) // group].wait()
        first_substep(z)
    for z in range(levels):
        second_substep(z)

    sends = []
    if early:
        first = levels // group - 1
        at = field_count - early
        block = second_ref[pl.ds(at, early), pl.ds(first * group, group)].reshape(early * group * width, owned)
        moved = picked(early_picks, block)
        for e in range(early):
            rows = moved[:, e * owned:(e + 1) * owned].reshape(devices, capacity, owned)
            early_ref[:, e * capacity:(e + 1) * capacity, :] = rows
        half = devices // 2
        sends.append(fetch(early_ref.at[pl.ds(half, half)], far_hbm, early_sem.at[0]))
        sends.append(fetch(early_ref.at[pl.ds(0, half)], near_hbm, early_sem.at[1]))
    group_rows = field_count * capacity
    aligned = group_rows % 8 == 0
    for number in range(levels // group):
        held = field_count - (early if number == levels // group - 1 else 0)
        blocks = second_ref[pl.ds(0, held), pl.ds(number * group, group)].reshape(held * group * width, owned)
        moved = picked(picks, blocks)
        for f in range(held):
            at = (number * field_count + f) * capacity
            send_ref[:, at:at + capacity, :] = moved[:, f * owned:(f + 1) * owned].reshape(devices, capacity, owned)
        if aligned:
            part = pl.ds(number * group_rows, held * capacity)
            sends.append(fetch(send_ref.at[:, part], send_hbm.at[:, part], send_sem.at[number]))
    if not aligned:
        sends.append(fetch(send_ref, send_hbm, send_sem.at[0]))

    tend_ref[...] = jnp.zeros_like(tend_ref)
    for f in range(field_count):
        for z in range(levels):
            gained = jnp.sum(second_ref[f, z] - crm_ref[f, z], axis=0, keepdims=True) * (1.0 / width)
            tend_ref[pl.ds(f * levels + z, 1), :] = gained
    small[3].wait()
    mass = mass_ref[...]
    fields = jnp.concatenate(
        [gcm_ref[f] for f in range(field_count)] + [mass, jnp.zeros((nodes, nodes - used - levels), jnp.float32)],
        axis=1,
    )
    factors = jnp.concatenate([mass] * field_count + [jnp.ones((nodes, nodes - used), jnp.float32)], axis=1)
    nodes_ref[...] = (fields + tend_ref[...].T) * factors
    return sends


def edges_y(elx, ely, side, nodes_ref, low_ref, high_ref):
    step = side * side
    for a in range(elx):
        first = a * ely * step
        final = (a * ely + ely - 1) * step + side - 1
        low_ref[a * side:(a + 1) * side, :] = nodes_ref[pl.ds(first, side, stride=side), :]
        high_ref[a * side:(a + 1) * side, :] = nodes_ref[pl.ds(final, side, stride=side), :]


def kernel_a(devices, capacity, early, elx, ely, side, *refs):
    sends = cloud_kernel(devices, capacity, early, *refs)
    edges_y(elx, ely, side, *refs[9:12])
    for copy in sends:
        copy.wait()


def divided(rows, levels, field, fields):
    mass = rows[:, fields * levels:(fields + 1) * levels]
    return rows[:, field * levels:(field + 1) * levels] / mass


def face_rows(elx, ely, side):
    step = side * side
    low = [b * step for b in range(ely)]
    return low, [((elx - 1) * ely + b) * step + (side - 1) * side for b in range(ely)]


def kernel_y(elx, ely, side, nodes_ref, south_ref, north_ref, part_ref, low_ref, high_ref, sum_ref, full_ref):
    step = side * side
    field_count, _, levels = part_ref.shape
    sum_ref[...] = nodes_ref[...]
    for a in range(elx):
        for b in range(ely):
            base = (a * ely + b) * step
            if b > 0:
                gain = nodes_ref[pl.ds(base - step + side - 1, side, stride=side), :]
            else:
                gain = south_ref[a * side:(a + 1) * side, :]
            here = pl.ds(base, side, stride=side)
            sum_ref[here, :] = nodes_ref[here, :] + gain
            if b + 1 < ely:
                gain = nodes_ref[pl.ds(base + step, side, stride=side), :]
            else:
                gain = north_ref[a * side:(a + 1) * side, :]
            here = pl.ds(base + side - 1, side, stride=side)
            sum_ref[here, :] = nodes_ref[here, :] + gain
    for face_ref, starts in zip((low_ref, high_ref), face_rows(elx, ely, side)):
        for b, start in enumerate(starts):
            face_ref[b * side:(b + 1) * side, :] = sum_ref[start:start + side, :]
    full_ref[...] = sum_ref[...]
    for a in range(elx - 1):
        for b in range(ely):
            last = (a * ely + b) * step + (side - 1) * side
            after = ((a + 1) * ely + b) * step
            joined = sum_ref[last:last + side, :] + sum_ref[after:after + side, :]
            full_ref[last:last + side, :] = joined
            full_ref[after:after + side, :] = joined
    full = full_ref[...]
    for f in range(field_count):
        part_ref[f] = divided(full, levels, f, field_count)


def complete_faces(elx, ely, side, low_ref, high_ref, west_ref, east_ref, gcm_ref):
    field_count, _, levels = gcm_ref.shape
    lows, highs = face_rows(elx, ely, side)
    for own_ref, sent_ref, starts in ((low_ref, west_ref, lows), (high_ref, east_ref, highs)):
        rows = own_ref[...] + sent_ref[...]
        for f in range(field_count):
            quotient = divided(rows, levels, f, field_count)
            for b, start in enumerate(starts):
                gcm_ref[f, start:start + side, :] = quotient[b * side:(b + 1) * side]


def turned_blocks(rows_of, out_hbm, out_ref, sem):
    block = out_ref.shape[0] // len(rows_of)
    copies = []
    for number, (step, slots_at) in enumerate(rows_of):
        here, there = pl.ds(number * block, block), pl.ds(step * block, block)
        out_ref[here, :] = slots_at().T
        copies.append(fetch(out_ref.at[here], out_hbm.at[there], sem.at[number]))
    return copies


def kernel_out(devices, capacity, groups, field_count, early, sizes, recv_ref, part_ref, west_ref, east_ref,
               low_ref, high_ref, *refs):
    out_hbm, gcm_hbm, out_ref, gcm_ref, spread_ref, sem, gcm_sem = refs[-7:]
    gcm_ref[...] = part_ref[...]
    complete_faces(*sizes, low_ref, high_ref, west_ref, east_ref, gcm_ref)
    gcm_copy = fetch(gcm_ref, gcm_hbm, gcm_sem)
    pitch = recv_ref.shape[0] // devices

    rows_ref = recv_ref
    if pitch % 16 == 0:
        rows_ref = spread_ref
        for source in range(devices):
            spread_ref[pl.ds(source * (pitch + 8), pitch), :] = recv_ref[pl.ds(source * pitch, pitch), :]
        pitch = pitch + 8

    def rows(first):
        ranked = [rows_ref[pl.ds(first + r, devices, stride=pitch), :] for r in range(capacity)]
        return jnp.concatenate(ranked, axis=0)

    blocks = groups * field_count - early
    steps = [(at % field_count) * groups + at // field_count for at in range(blocks)]
    rows_of = [(step, functools.partial(rows, at * capacity)) for at, step in enumerate(steps)]
    for copy in [gcm_copy] + turned_blocks(rows_of, out_hbm, out_ref, sem):
        copy.wait()


def kernel_early(devices, capacity, groups, field_count, early, sources, me_ref, *refs):
    apart = devices + 8
    slots = apart * capacity
    *blocks, out_hbm, row_ref, out_ref, sem = refs
    arrived = [(ref, index) for ref in blocks for index in range(ref.shape[0])]
    for (ref, index), bits in zip(arrived, sources):
        for e in range(early):
            tile = ref[index, pl.ds(e * capacity, capacity), :]
            row_ref[pl.ds(e * slots + (me_ref[0] ^ bits), capacity, stride=apart), :] = tile
    steps = [(field_count - early + e) * groups + groups - 1 for e in range(early)]

    def slots_at(first):
        ranked = [row_ref[first + r * apart:first + r * apart + devices, :] for r in range(capacity)]
        return jnp.concatenate(ranked, axis=0)

    rows_of = [(step, functools.partial(slots_at, e * slots)) for e, step in enumerate(steps)]
    for copy in turned_blocks(rows_of, out_hbm, out_ref, sem):
        copy.wait()


def params(mib):
    return pltpu.CompilerParams(vmem_limit_bytes=mib * MIB)


def cost(flops, byte_count):
    return pl.CostEstimate(flops=flops, bytes_accessed=byte_count, transcendentals=0)


def shift(face, axis, by):
    count = lax.axis_size(axis)
    return lax.ppermute(face, axis, [(i, (i + by) % count) for i in range(count)])


def exchange(block, bits):
    count = lax.axis_size(AXES)
    return lax.ppermute(block, AXES, [(i, i ^ bits) for i in range(count)])


def kernel_regroup(kept_ref, last_ref, *out_refs):
    count = kept_ref.shape[1] // len(out_refs)
    for number, out_ref in enumerate(out_refs):
        part = pl.ds(number * count, count)
        out_ref[0:1] = kept_ref[:, part]
        out_ref[1:2] = last_ref[:, part]


def regrouped(arrays, ways, first):
    count = arrays[0].shape[1] // ways
    if first:
        shape = jax.ShapeDtypeStruct((2, count) + arrays[0].shape[2:], arrays[0].dtype)
        return pl.pallas_call(
            kernel_regroup,
            out_shape=[shape] * ways,
            compiler_params=params(8),
            cost_estimate=cost(REGROUP_FLOPS, 10**6),
            name="regroup",
        )(*arrays)
    return [jnp.concatenate([a[:, i * count:(i + 1) * count] for a in arrays]) for i in range(ways)]


def hops(near, far, devices):
    top, *others = hop_bits(devices)
    arrays = [near[None], exchange(far, 1 << top)[None]]
    senders = [0, 1 << top]
    middle = len(others) - 1
    steps = [others[:1], others[1:middle], others[middle:]]
    for step in steps:
        moves = [0]
        for bit in step:
            moves = [move | flip for move in moves for flip in (0, 1 << bit)]
        parts = regrouped(arrays, len(moves), step is steps[0])
        arrays = [exchange(part, move) if move else part for part, move in zip(parts, moves)]
        senders = [sender ^ move for move in moves for sender in senders]
    return [array[:, 0] for array in arrays], senders


def body(crm_state, gcm_state, mass, dest, cost_class):
    devices = lax.axis_size(("ex", "ey"))
    field_count, levels, width, owned = crm_state.shape
    elx, ely, side = gcm_state.shape[2:5]
    capacity = max(2, 2 * owned // devices)
    slots = capacity * devices
    values = field_count * levels * width
    f32 = jnp.float32
    gcm_nodes = gcm_state.transpose(0, 2, 3, 4, 5, 1).reshape(field_count, owned, levels)
    mass_nodes = mass.transpose(1, 2, 3, 4, 0).reshape(owned, levels)
    sizes = (elx, ely, side)
    face_x = jax.ShapeDtypeStruct((ely * side, owned), f32)
    face_y = jax.ShapeDtypeStruct((elx * side, owned), f32)
    in_hbm = pl.BlockSpec(memory_space=pltpu.HBM)
    in_vmem = pl.BlockSpec(memory_space=pltpu.VMEM)
    square = jax.ShapeDtypeStruct((owned, owned), f32)
    in_smem = pl.BlockSpec(memory_space=pltpu.SMEM)
    me = lax.axis_index(AXES).astype(jnp.int32).reshape(1)
    groups = levels * width // owned
    early = EARLY_BLOCKS if capacity % 8 == 0 and devices & (devices - 1) == 0 else 0
    packed = (devices, (values // owned - early) * capacity, owned)
    apart = (max(2, devices) // 2, max(1, early) * capacity, owned)
    send, far, near, nodes, low, high = pl.pallas_call(
        functools.partial(kernel_a, devices, capacity, early, *sizes),
        out_shape=(
            jax.ShapeDtypeStruct(packed, f32),
            jax.ShapeDtypeStruct(apart, f32),
            jax.ShapeDtypeStruct(apart, f32),
            square,
            face_y,
            face_y,
        ),
        in_specs=[in_smem] + [in_hbm] * 5,
        out_specs=(in_hbm, in_hbm, in_hbm, in_vmem, in_vmem, in_vmem),
        scratch_shapes=[
            pltpu.VMEM(crm_state.shape, f32),
            pltpu.VMEM(crm_state.shape, f32),
            pltpu.VMEM((owned, owned), f32),
            pltpu.VMEM((owned, owned), f32),
            pltpu.VMEM(crm_state.shape, f32),
            pltpu.VMEM(gcm_nodes.shape, f32),
            pltpu.VMEM(mass_nodes.shape, f32),
            pltpu.VMEM((1, owned), jnp.int32),
            pltpu.VMEM((1, owned), jnp.int32),
            pltpu.VMEM(packed, f32),
            pltpu.VMEM((devices,) + apart[1:], f32),
            pltpu.SemaphoreType.DMA((4,)),
            pltpu.SemaphoreType.DMA((groups,)),
            pltpu.SemaphoreType.DMA((groups,)),
            pltpu.SemaphoreType.DMA((2,)),
        ],
        compiler_params=params(63),
        name="cloud_models",
    )(me, crm_state, gcm_nodes, mass_nodes, dest.reshape(1, owned), cost_class.reshape(1, owned))
    received = lax.all_to_all(send, AXES, split_axis=0, concat_axis=0, tiled=True)
    if early:
        arrived, sources = hops(near, far, devices)
    north = shift(low, "ey", -1)
    south = shift(high, "ey", 1)
    part, low, high = pl.pallas_call(
        functools.partial(kernel_y, *sizes),
        out_shape=(jax.ShapeDtypeStruct((field_count, owned, levels), f32), face_x, face_x),
        scratch_shapes=[pltpu.VMEM((owned, owned), f32)] * 2,
        compiler_params=params(8),
        cost_estimate=cost(10**9, 10**5),
        name="edge_sum_second",
    )(nodes, south, north)
    east = shift(low, "ex", -1)
    west = shift(high, "ex", 1)
    if early:
        part, arrived[-1] = lax.optimization_barrier((part, arrived[-1]))
    out_shape = jax.ShapeDtypeStruct((values, slots), f32)
    block_count = values // owned
    begun = []
    if early:
        begun.append(pl.pallas_call(
            functools.partial(kernel_early, devices, capacity, groups, field_count, early, sources),
            in_specs=[in_smem] + [in_vmem] * len(arrived),
            out_specs=in_hbm,
            out_shape=out_shape,
            scratch_shapes=[
                pltpu.VMEM((early * (devices + 8) * capacity, owned), f32),
                pltpu.VMEM((early * owned, slots), f32),
                pltpu.SemaphoreType.DMA((early,)),
            ],
            compiler_params=params(8),
            cost_estimate=cost(EARLY_FLOPS, 10**6),
            name="early_slots",
        )(me, *arrived))
    cloud, gcm_out = pl.pallas_call(
        functools.partial(kernel_out, devices, capacity, groups, field_count, early, sizes),
        in_specs=[in_vmem] * 6 + [in_hbm] * len(begun),
        out_specs=(in_hbm, in_hbm),
        out_shape=(out_shape, jax.ShapeDtypeStruct((field_count, owned, levels), f32)),
        input_output_aliases={6: 0} if begun else {},
        scratch_shapes=[
            pltpu.VMEM(((block_count - early) * owned, slots), f32),
            pltpu.VMEM((field_count, owned, levels), f32),
            pltpu.VMEM((devices * ((block_count - early) * capacity + 8), owned), f32),
            pltpu.SemaphoreType.DMA((block_count - early,)),
            pltpu.SemaphoreType.DMA,
        ],
        compiler_params=params(16),
        name="cloud_slots",
    )(received.reshape(-1, owned), part, west, east, low, high, *begun)
    gcm_out = gcm_out.reshape(field_count, elx, ely, side, side, levels).transpose(0, 5, 1, 2, 3, 4)
    return cloud.reshape(field_count, levels, width, slots), gcm_out


def solution(mesh):
    return jax.shard_map(
        body,
        mesh=mesh,
        in_specs=(
            P(None, None, None, ("ex", "ey")),
            P(None, None, "ex", "ey", None, None),
            P(None, "ex", "ey", None, None),
            P(("ex", "ey"), None),
            P(("ex", "ey")),
        ),
        out_specs=(P(None, None, None, ("ex", "ey")), P(None, None, "ex", "ey", None, None)),
        check_vma=False,
    )
```

```python
import functools

import jax
import jax.numpy as jnp
from jax import lax
from jax.experimental import pallas as pl
from jax.experimental.pallas import tpu as pltpu
from jax.sharding import PartitionSpec as P

diffusion = 0.1
advection = 0.15
buoyancy = 0.3
latent_heat = 0.5
fallout = 0.2
condense_rate = 0.4
nudging = 0.5

AXES = ("ex", "ey")
NT = (((1,), (1,)), ((), ()))
MIB = 1024 * 1024
REGROUP_FLOPS = 6*10**9
EARLY_BLOCKS = 3
EARLY_FLOPS = 13*10**9


def substep_level(values_at, nudge_row, z, levels, field_count, active=None):
    values = [values_at(f, z) for f in range(field_count)]
    width = values[0].shape[0]
    drift = (advection * 0.5) * values[0]
    from_east, from_west = diffusion - drift, diffusion + drift
    condensed = condense_rate * jnp.maximum(values[3], 0.0)
    results = []
    for f in range(field_count):
        v = values[f]
        east = pltpu.roll(v, width - 1, 0)
        west = pltpu.roll(v, 1, 0)
        fresh = east * from_east + west * from_west
        if 0 < z < levels - 1:
            fresh = fresh + diffusion * (values_at(f, z + 1) + values_at(f, z - 1))
        else:
            fresh = fresh + diffusion * values_at(f, z + 1 if z == 0 else z - 1)
        fresh = fresh + (nudge_row(f, z) - (nudging / width) * jnp.sum(v, axis=0, keepdims=True))
        own = 1.0 - 4.0 * diffusion
        if f == 1:
            fresh = fresh + buoyancy * values[2]
        elif f == 2:
            fresh = fresh - buoyancy * values[1] + latent_heat * condensed
        elif f == 3:
            fresh = fresh - condensed
        elif f == 4:
            fresh = fresh + condensed
            own = own - fallout
        fresh = fresh + own * v
        results.append(fresh if active is None else jnp.where(active, fresh, v))
    return results


def slot_rank(dest):
    owned = dest.shape[1]
    named = jnp.broadcast_to(dest.astype(jnp.float32), (owned, owned))
    rows = lax.broadcasted_iota(jnp.int32, (owned, owned), 0)
    cols = lax.broadcasted_iota(jnp.int32, (owned, owned), 1)
    earlier = jnp.where((named == named.T) & (rows < cols), 1, 0)
    return jnp.sum(earlier, axis=0, keepdims=True)


def one_hot_rows(slot, count):
    rows = lax.broadcasted_iota(jnp.int32, (count, slot.shape[1]), 0)
    return jnp.concatenate([jnp.where(rows == slot, 1.0, 0.0).astype(jnp.bfloat16)] * 3, axis=1)


def hop_bits(devices):
    bits = devices.bit_length() - 1
    return [bits - 1] + list(range(bits - 1))


def hop_order(difference, devices):
    place = jnp.zeros_like(difference)
    for bit in hop_bits(devices):
        place = 2 * place + ((difference >> bit) & 1)
    return place


def picked(picks, block):
    high = block.astype(jnp.bfloat16)
    rest = block - high.astype(jnp.float32)
    middle = rest.astype(jnp.bfloat16)
    low = (rest - middle.astype(jnp.float32)).astype(jnp.bfloat16)
    parts = jnp.concatenate([high, middle, low], axis=1)
    return lax.dot_general(picks, parts, NT, preferred_element_type=jnp.float32)


def fetch(source, target, sem):
    copy = pltpu.make_async_copy(source, target, sem)
    copy.start()
    return copy


def cloud_kernel(devices, capacity, early, me_ref, crm_hbm, gcm_hbm, mass_hbm, dest_hbm, cost_hbm,
                 send_hbm, far_hbm, near_hbm, nodes_ref, low_ref, high_ref, first_ref, second_ref, prof_ref, tend_ref,
                 crm_ref, gcm_ref, mass_ref, dest_ref, cost_ref, send_ref, early_ref, small_sem, crm_sem, send_sem, early_sem):
    field_count, levels, width, owned = crm_ref.shape
    group = owned // width
    small = [
        fetch(dest_hbm, dest_ref, small_sem.at[0]),
        fetch(gcm_hbm, gcm_ref, small_sem.at[1]),
        fetch(cost_hbm, cost_ref, small_sem.at[2]),
    ]
    pieces = [
        fetch(crm_hbm.at[:, pl.ds(z, group)], crm_ref.at[:, pl.ds(z, group)], crm_sem.at[z // group])
        for z in range(0, levels, group)
    ]
    small.append(fetch(mass_hbm, mass_ref, small_sem.at[3]))
    used = field_count * levels
    nodes = gcm_ref.shape[1]

    small[0].wait()
    rank = slot_rank(dest_ref[...])
    picks = one_hot_rows(dest_ref[...] * capacity + rank, devices * capacity)
    if early:
        turned = hop_order(dest_ref[...] ^ me_ref[0], devices)
        early_picks = one_hot_rows(turned * capacity + rank, devices * capacity)
    small[1].wait()
    grid_fields = jnp.concatenate(
        [gcm_ref[f] for f in range(field_count)] + [jnp.zeros((nodes, nodes - used), jnp.float32)], axis=1
    )
    prof_ref[...] = nudging * grid_fields.T
    small[2].wait()
    twice = jnp.broadcast_to(cost_ref[...] >= 2, (width, owned))

    def nudge_row(f, z):
        return prof_ref[pl.ds(f * levels + z, 1), :]

    def first_substep(z):
        fresh = substep_level(lambda f, k: crm_ref[f, k], nudge_row, z, levels, field_count)
        for f in range(field_count):
            first_ref[f, z] = fresh[f]

    def second_substep(z):
        fresh = substep_level(lambda f, k: first_ref[f, k], nudge_row, z, levels, field_count, twice)
        for f in range(field_count):
            second_ref[f, z] = fresh[f]

    pieces[0].wait()
    for z in range(levels):
        if (z + 1) % group == 0 and z + 1 < levels:
            pieces[(z + 1) // group].wait()
        first_substep(z)
    for z in range(levels):
        second_substep(z)

    sends = []
    if early:
        first = levels // group - 1
        at = field_count - early
        block = second_ref[pl.ds(at, early), pl.ds(first * group, group)].reshape(early * group * width, owned)
        moved = picked(early_picks, block)
        for e in range(early):
            rows = moved[:, e * owned:(e + 1) * owned].reshape(devices, capacity, owned)
            early_ref[:, e * capacity:(e + 1) * capacity, :] = rows
        half = devices // 2
        sends.append(fetch(early_ref.at[pl.ds(half, half)], far_hbm, early_sem.at[0]))
        sends.append(fetch(early_ref.at[pl.ds(0, half)], near_hbm, early_sem.at[1]))
    group_rows = field_count * capacity
    aligned = group_rows % 8 == 0
    for number in range(levels // group):
        held = field_count - (early if number == levels // group - 1 else 0)
        blocks = second_ref[pl.ds(0, held), pl.ds(number * group, group)].reshape(held * group * width, owned)
        moved = picked(picks, blocks)
        for f in range(held):
            at = (number * field_count + f) * capacity
            send_ref[:, at:at + capacity, :] = moved[:, f * owned:(f + 1) * owned].reshape(devices, capacity, owned)
        if aligned:
            part = pl.ds(number * group_rows, held * capacity)
            sends.append(fetch(send_ref.at[:, part], send_hbm.at[:, part], send_sem.at[number]))
    if not aligned:
        sends.append(fetch(send_ref, send_hbm, send_sem.at[0]))

    tend_ref[...] = jnp.zeros_like(tend_ref)
    for f in range(field_count):
        for z in range(levels):
            gained = jnp.sum(second_ref[f, z] - crm_ref[f, z], axis=0, keepdims=True) * (1.0 / width)
            tend_ref[pl.ds(f * levels + z, 1), :] = gained
    small[3].wait()
    mass = mass_ref[...]
    fields = jnp.concatenate(
        [gcm_ref[f] for f in range(field_count)] + [mass, jnp.zeros((nodes, nodes - used - levels), jnp.float32)],
        axis=1,
    )
    factors = jnp.concatenate([mass] * field_count + [jnp.ones((nodes, nodes - used), jnp.float32)], axis=1)
    nodes_ref[...] = (fields + tend_ref[...].T) * factors
    return sends


def edges_y(elx, ely, side, nodes_ref, low_ref, high_ref):
    step = side * side
    for a in range(elx):
        first = a * ely * step
        final = (a * ely + ely - 1) * step + side - 1
        low_ref[a * side:(a + 1) * side, :] = nodes_ref[pl.ds(first, side, stride=side), :]
        high_ref[a * side:(a + 1) * side, :] = nodes_ref[pl.ds(final, side, stride=side), :]


def kernel_a(devices, capacity, early, elx, ely, side, *refs):
    sends = cloud_kernel(devices, capacity, early, *refs)
    edges_y(elx, ely, side, *refs[9:12])
    for copy in sends:
        copy.wait()


def divided(rows, levels, field, fields):
    mass = rows[:, fields * levels:(fields + 1) * levels]
    return rows[:, field * levels:(field + 1) * levels] / mass


def face_rows(elx, ely, side):
    step = side * side
    low = [b * step for b in range(ely)]
    return low, [((elx - 1) * ely + b) * step + (side - 1) * side for b in range(ely)]


def kernel_y(elx, ely, side, nodes_ref, south_ref, north_ref, part_ref, low_ref, high_ref, sum_ref, full_ref):
    step = side * side
    field_count, _, levels = part_ref.shape
    sum_ref[...] = nodes_ref[...]
    for a in range(elx):
        for b in range(ely):
            base = (a * ely + b) * step
            if b > 0:
                gain = nodes_ref[pl.ds(base - step + side - 1, side, stride=side), :]
            else:
                gain = south_ref[a * side:(a + 1) * side, :]
            here = pl.ds(base, side, stride=side)
            sum_ref[here, :] = nodes_ref[here, :] + gain
            if b + 1 < ely:
                gain = nodes_ref[pl.ds(base + step, side, stride=side), :]
            else:
                gain = north_ref[a * side:(a + 1) * side, :]
            here = pl.ds(base + side - 1, side, stride=side)
            sum_ref[here, :] = nodes_ref[here, :] + gain
    for face_ref, starts in zip((low_ref, high_ref), face_rows(elx, ely, side)):
        for b, start in enumerate(starts):
            face_ref[b * side:(b + 1) * side, :] = sum_ref[start:start + side, :]
    full_ref[...] = sum_ref[...]
    for a in range(elx - 1):
        for b in range(ely):
            last = (a * ely + b) * step + (side - 1) * side
            after = ((a + 1) * ely + b) * step
            joined = sum_ref[last:last + side, :] + sum_ref[after:after + side, :]
            full_ref[last:last + side, :] = joined
            full_ref[after:after + side, :] = joined
    full = full_ref[...]
    for f in range(field_count):
        part_ref[f] = divided(full, levels, f, field_count)


def complete_faces(elx, ely, side, low_ref, high_ref, west_ref, east_ref, gcm_ref):
    field_count, _, levels = gcm_ref.shape
    lows, highs = face_rows(elx, ely, side)
    for own_ref, sent_ref, starts in ((low_ref, west_ref, lows), (high_ref, east_ref, highs)):
        rows = own_ref[...] + sent_ref[...]
        for f in range(field_count):
            quotient = divided(rows, levels, f, field_count)
            for b, start in enumerate(starts):
                gcm_ref[f, start:start + side, :] = quotient[b * side:(b + 1) * side]


def turned_blocks(rows_of, out_hbm, out_ref, sem):
    block = out_ref.shape[0] // len(rows_of)
    copies = []
    for number, (step, slots_at) in enumerate(rows_of):
        here, there = pl.ds(number * block, block), pl.ds(step * block, block)
        out_ref[here, :] = slots_at().T
        copies.append(fetch(out_ref.at[here], out_hbm.at[there], sem.at[number]))
    return copies


def kernel_out(devices, capacity, groups, field_count, early, sizes, recv_ref, part_ref, west_ref, east_ref,
               low_ref, high_ref, *refs):
    out_hbm, gcm_hbm, out_ref, gcm_ref, spread_ref, sem, gcm_sem = refs[-7:]
    gcm_ref[...] = part_ref[...]
    complete_faces(*sizes, low_ref, high_ref, west_ref, east_ref, gcm_ref)
    gcm_copy = fetch(gcm_ref, gcm_hbm, gcm_sem)
    pitch = recv_ref.shape[0] // devices

    slots = devices * capacity

    def rows(first):
        if pitch % 16:
            ranked = [recv_ref[pl.ds(first + r, devices, stride=pitch), :] for r in range(capacity)]
            return jnp.concatenate(ranked, axis=0)
        base = first // capacity * slots
        for source in range(devices):
            tile = recv_ref[pl.ds(source * pitch + first, capacity), :]
            spread_ref[pl.ds(base + source * capacity, capacity), :] = tile
        ranked = [spread_ref[pl.ds(base + r, devices, stride=capacity), :] for r in range(capacity)]
        return jnp.concatenate(ranked, axis=0)

    blocks = groups * field_count - early
    steps = [(at % field_count) * groups + at // field_count for at in range(blocks)]
    rows_of = [(step, functools.partial(rows, at * capacity)) for at, step in enumerate(steps)]
    for copy in [gcm_copy] + turned_blocks(rows_of, out_hbm, out_ref, sem):
        copy.wait()


def kernel_early(devices, capacity, groups, field_count, early, sources, me_ref, *refs):
    apart = devices + 8
    slots = apart * capacity
    *blocks, out_hbm, row_ref, out_ref, sem = refs
    arrived = [(ref, index) for ref in blocks for index in range(ref.shape[0])]
    for (ref, index), bits in zip(arrived, sources):
        for e in range(early):
            tile = ref[index, pl.ds(e * capacity, capacity), :]
            row_ref[pl.ds(e * slots + (me_ref[0] ^ bits), capacity, stride=apart), :] = tile
    steps = [(field_count - early + e) * groups + groups - 1 for e in range(early)]

    def slots_at(first):
        ranked = [row_ref[first + r * apart:first + r * apart + devices, :] for r in range(capacity)]
        return jnp.concatenate(ranked, axis=0)

    rows_of = [(step, functools.partial(slots_at, e * slots)) for e, step in enumerate(steps)]
    for copy in turned_blocks(rows_of, out_hbm, out_ref, sem):
        copy.wait()


def params(mib):
    return pltpu.CompilerParams(vmem_limit_bytes=mib * MIB)


def cost(flops, byte_count):
    return pl.CostEstimate(flops=flops, bytes_accessed=byte_count, transcendentals=0)


def shift(face, axis, by):
    count = lax.axis_size(axis)
    return lax.ppermute(face, axis, [(i, (i + by) % count) for i in range(count)])


def exchange(block, bits):
    count = lax.axis_size(AXES)
    return lax.ppermute(block, AXES, [(i, i ^ bits) for i in range(count)])


def kernel_regroup(kept_ref, last_ref, *out_refs):
    count = kept_ref.shape[1] // len(out_refs)
    for number, out_ref in enumerate(out_refs):
        part = pl.ds(number * count, count)
        out_ref[0:1] = kept_ref[:, part]
        out_ref[1:2] = last_ref[:, part]


def regrouped(arrays, ways, first):
    count = arrays[0].shape[1] // ways
    if first:
        shape = jax.ShapeDtypeStruct((2, count) + arrays[0].shape[2:], arrays[0].dtype)
        return pl.pallas_call(
            kernel_regroup,
            out_shape=[shape] * ways,
            compiler_params=params(8),
            cost_estimate=cost(REGROUP_FLOPS, 10**6),
            name="regroup",
        )(*arrays)
    return [jnp.concatenate([a[:, i * count:(i + 1) * count] for a in arrays]) for i in range(ways)]


def hops(near, far, devices):
    top, *others = hop_bits(devices)
    arrays = [near[None], exchange(far, 1 << top)[None]]
    senders = [0, 1 << top]
    middle = len(others) - 1
    steps = [others[:1], others[1:middle], others[middle:]]
    for step in steps:
        moves = [0]
        for bit in step:
            moves = [move | flip for move in moves for flip in (0, 1 << bit)]
        parts = regrouped(arrays, len(moves), step is steps[0])
        arrays = [exchange(part, move) if move else part for part, move in zip(parts, moves)]
        senders = [sender ^ move for move in moves for sender in senders]
    return [array[:, 0] for array in arrays], senders


def body(crm_state, gcm_state, mass, dest, cost_class):
    devices = lax.axis_size(("ex", "ey"))
    field_count, levels, width, owned = crm_state.shape
    elx, ely, side = gcm_state.shape[2:5]
    capacity = max(2, 2 * owned // devices)
    slots = capacity * devices
    values = field_count * levels * width
    f32 = jnp.float32
    gcm_nodes = gcm_state.transpose(0, 2, 3, 4, 5, 1).reshape(field_count, owned, levels)
    mass_nodes = mass.transpose(1, 2, 3, 4, 0).reshape(owned, levels)
    sizes = (elx, ely, side)
    face_x = jax.ShapeDtypeStruct((ely * side, owned), f32)
    face_y = jax.ShapeDtypeStruct((elx * side, owned), f32)
    in_hbm = pl.BlockSpec(memory_space=pltpu.HBM)
    in_vmem = pl.BlockSpec(memory_space=pltpu.VMEM)
    square = jax.ShapeDtypeStruct((owned, owned), f32)
    in_smem = pl.BlockSpec(memory_space=pltpu.SMEM)
    me = lax.axis_index(AXES).astype(jnp.int32).reshape(1)
    groups = levels * width // owned
    early = EARLY_BLOCKS if capacity % 8 == 0 and devices & (devices - 1) == 0 else 0
    packed = (devices, (values // owned - early) * capacity, owned)
    apart = (max(2, devices) // 2, max(1, early) * capacity, owned)
    send, far, near, nodes, low, high = pl.pallas_call(
        functools.partial(kernel_a, devices, capacity, early, *sizes),
        out_shape=(
            jax.ShapeDtypeStruct(packed, f32),
            jax.ShapeDtypeStruct(apart, f32),
            jax.ShapeDtypeStruct(apart, f32),
            square,
            face_y,
            face_y,
        ),
        in_specs=[in_smem] + [in_hbm] * 5,
        out_specs=(in_hbm, in_hbm, in_hbm, in_vmem, in_vmem, in_vmem),
        scratch_shapes=[
            pltpu.VMEM(crm_state.shape, f32),
            pltpu.VMEM(crm_state.shape, f32),
            pltpu.VMEM((owned, owned), f32),
            pltpu.VMEM((owned, owned), f32),
            pltpu.VMEM(crm_state.shape, f32),
            pltpu.VMEM(gcm_nodes.shape, f32),
            pltpu.VMEM(mass_nodes.shape, f32),
            pltpu.VMEM((1, owned), jnp.int32),
            pltpu.VMEM((1, owned), jnp.int32),
            pltpu.VMEM(packed, f32),
            pltpu.VMEM((devices,) + apart[1:], f32),
            pltpu.SemaphoreType.DMA((4,)),
            pltpu.SemaphoreType.DMA((groups,)),
            pltpu.SemaphoreType.DMA((groups,)),
            pltpu.SemaphoreType.DMA((2,)),
        ],
        compiler_params=params(63),
        name="cloud_models",
    )(me, crm_state, gcm_nodes, mass_nodes, dest.reshape(1, owned), cost_class.reshape(1, owned))
    received = lax.all_to_all(send, AXES, split_axis=0, concat_axis=0, tiled=True)
    if early:
        arrived, sources = hops(near, far, devices)
    north = shift(low, "ey", -1)
    south = shift(high, "ey", 1)
    part, low, high = pl.pallas_call(
        functools.partial(kernel_y, *sizes),
        out_shape=(jax.ShapeDtypeStruct((field_count, owned, levels), f32), face_x, face_x),
        scratch_shapes=[pltpu.VMEM((owned, owned), f32)] * 2,
        compiler_params=params(8),
        cost_estimate=cost(10**9, 10**5),
        name="edge_sum_second",
    )(nodes, south, north)
    east = shift(low, "ex", -1)
    west = shift(high, "ex", 1)
    if early:
        part, arrived[-1] = lax.optimization_barrier((part, arrived[-1]))
    out_shape = jax.ShapeDtypeStruct((values, slots), f32)
    block_count = values // owned
    begun = []
    if early:
        begun.append(pl.pallas_call(
            functools.partial(kernel_early, devices, capacity, groups, field_count, early, sources),
            in_specs=[in_smem] + [in_vmem] * len(arrived),
            out_specs=in_hbm,
            out_shape=out_shape,
            scratch_shapes=[
                pltpu.VMEM((early * (devices + 8) * capacity, owned), f32),
                pltpu.VMEM((early * owned, slots), f32),
                pltpu.SemaphoreType.DMA((early,)),
            ],
            compiler_params=params(8),
            cost_estimate=cost(EARLY_FLOPS, 10**6),
            name="early_slots",
        )(me, *arrived))
    cloud, gcm_out = pl.pallas_call(
        functools.partial(kernel_out, devices, capacity, groups, field_count, early, sizes),
        in_specs=[in_vmem] * 6 + [in_hbm] * len(begun),
        out_specs=(in_hbm, in_hbm),
        out_shape=(out_shape, jax.ShapeDtypeStruct((field_count, owned, levels), f32)),
        input_output_aliases={6: 0} if begun else {},
        scratch_shapes=[
            pltpu.VMEM(((block_count - early) * owned, slots), f32),
            pltpu.VMEM((field_count, owned, levels), f32),
            pltpu.VMEM((devices * ((block_count - early) * capacity + 8), owned), f32),
            pltpu.SemaphoreType.DMA((block_count - early,)),
            pltpu.SemaphoreType.DMA,
        ],
        compiler_params=params(16),
        name="cloud_slots",
    )(received.reshape(-1, owned), part, west, east, low, high, *begun)
    gcm_out = gcm_out.reshape(field_count, elx, ely, side, side, levels).transpose(0, 5, 1, 2, 3, 4)
    return cloud.reshape(field_count, levels, width, slots), gcm_out


def solution(mesh):
    return jax.shard_map(
        body,
        mesh=mesh,
        in_specs=(
            P(None, None, None, ("ex", "ey")),
            P(None, None, "ex", "ey", None, None),
            P(None, "ex", "ey", None, None),
            P(("ex", "ey"), None),
            P(("ex", "ey")),
        ),
        out_specs=(P(None, None, None, ("ex", "ey")), P(None, None, "ex", "ey", None, None)),
        check_vma=False,
    )
```

```python
import functools

import jax
import jax.numpy as jnp
from jax import lax
from jax.experimental import pallas as pl
from jax.experimental.pallas import tpu as pltpu
from jax.sharding import PartitionSpec as P

diffusion = 0.1
advection = 0.15
buoyancy = 0.3
latent_heat = 0.5
fallout = 0.2
condense_rate = 0.4
nudging = 0.5

AXES = ("ex", "ey")
NT = (((1,), (1,)), ((), ()))
MIB = 1024 * 1024
REGROUP_FLOPS = 6*10**9
EARLY_BLOCKS = 3
EARLY_FLOPS = 13*10**9


def substep_level(values_at, nudge_row, z, levels, field_count, active=None):
    values = [values_at(f, z) for f in range(field_count)]
    width = values[0].shape[0]
    drift = (advection * 0.5) * values[0]
    from_east, from_west = diffusion - drift, diffusion + drift
    condensed = condense_rate * jnp.maximum(values[3], 0.0)
    results = []
    for f in range(field_count):
        v = values[f]
        east = pltpu.roll(v, width - 1, 0)
        west = pltpu.roll(v, 1, 0)
        fresh = east * from_east + west * from_west
        if 0 < z < levels - 1:
            fresh = fresh + diffusion * (values_at(f, z + 1) + values_at(f, z - 1))
        else:
            fresh = fresh + diffusion * values_at(f, z + 1 if z == 0 else z - 1)
        fresh = fresh + (nudge_row(f, z) - (nudging / width) * jnp.sum(v, axis=0, keepdims=True))
        own = 1.0 - 4.0 * diffusion
        if f == 1:
            fresh = fresh + buoyancy * values[2]
        elif f == 2:
            fresh = fresh - buoyancy * values[1] + latent_heat * condensed
        elif f == 3:
            fresh = fresh - condensed
        elif f == 4:
            fresh = fresh + condensed
            own = own - fallout
        fresh = fresh + own * v
        results.append(fresh if active is None else jnp.where(active, fresh, v))
    return results


def slot_rank(dest):
    owned = dest.shape[1]
    named = jnp.broadcast_to(dest.astype(jnp.float32), (owned, owned))
    rows = lax.broadcasted_iota(jnp.int32, (owned, owned), 0)
    cols = lax.broadcasted_iota(jnp.int32, (owned, owned), 1)
    earlier = jnp.where((named == named.T) & (rows < cols), 1, 0)
    return jnp.sum(earlier, axis=0, keepdims=True)


def one_hot_rows(slot, count):
    rows = lax.broadcasted_iota(jnp.int32, (count, slot.shape[1]), 0)
    return jnp.concatenate([jnp.where(rows == slot, 1.0, 0.0).astype(jnp.bfloat16)] * 3, axis=1)


def hop_bits(devices):
    bits = devices.bit_length() - 1
    return [bits - 1] + list(range(bits - 1))


def hop_order(difference, devices):
    place = jnp.zeros_like(difference)
    for bit in hop_bits(devices):
        place = 2 * place + ((difference >> bit) & 1)
    return place


def picked(picks, block):
    high = block.astype(jnp.bfloat16)
    rest = block - high.astype(jnp.float32)
    middle = rest.astype(jnp.bfloat16)
    low = (rest - middle.astype(jnp.float32)).astype(jnp.bfloat16)
    parts = jnp.concatenate([high, middle, low], axis=1)
    return lax.dot_general(picks, parts, NT, preferred_element_type=jnp.float32)


def fetch(source, target, sem, priority=0):
    copy = pltpu.make_async_copy(source, target, sem)
    copy.start(priority=priority)
    return copy


def cloud_kernel(devices, capacity, early, me_ref, crm_hbm, gcm_hbm, mass_hbm, dest_hbm, cost_hbm,
                 send_hbm, far_hbm, near_hbm, nodes_ref, low_ref, high_ref, first_ref, second_ref, prof_ref, tend_ref,
                 crm_ref, gcm_ref, mass_ref, dest_ref, cost_ref, send_ref, early_ref, small_sem, crm_sem, send_sem, early_sem):
    field_count, levels, width, owned = crm_ref.shape
    group = owned // width
    small = [
        fetch(dest_hbm, dest_ref, small_sem.at[0]),
        fetch(gcm_hbm, gcm_ref, small_sem.at[1]),
        fetch(cost_hbm, cost_ref, small_sem.at[2]),
    ]
    pieces = [
        fetch(crm_hbm.at[:, pl.ds(z, group)], crm_ref.at[:, pl.ds(z, group)], crm_sem.at[z // group], 1)
        for z in range(0, levels, group)
    ]
    small.append(fetch(mass_hbm, mass_ref, small_sem.at[3]))
    used = field_count * levels
    nodes = gcm_ref.shape[1]

    small[0].wait()
    rank = slot_rank(dest_ref[...])
    picks = one_hot_rows(dest_ref[...] * capacity + rank, devices * capacity)
    if early:
        turned = hop_order(dest_ref[...] ^ me_ref[0], devices)
        early_picks = one_hot_rows(turned * capacity + rank, devices * capacity)
    small[1].wait()
    grid_fields = jnp.concatenate(
        [gcm_ref[f] for f in range(field_count)] + [jnp.zeros((nodes, nodes - used), jnp.float32)], axis=1
    )
    prof_ref[...] = nudging * grid_fields.T
    small[2].wait()
    twice = jnp.broadcast_to(cost_ref[...] >= 2, (width, owned))

    def nudge_row(f, z):
        return prof_ref[pl.ds(f * levels + z, 1), :]

    def first_substep(z):
        fresh = substep_level(lambda f, k: crm_ref[f, k], nudge_row, z, levels, field_count)
        for f in range(field_count):
            first_ref[f, z] = fresh[f]

    def second_substep(z):
        fresh = substep_level(lambda f, k: first_ref[f, k], nudge_row, z, levels, field_count, twice)
        for f in range(field_count):
            second_ref[f, z] = fresh[f]

    pieces[0].wait()
    for z in range(levels):
        if (z + 1) % group == 0 and z + 1 < levels:
            pieces[(z + 1) // group].wait()
        first_substep(z)
    for z in range(levels):
        second_substep(z)

    sends = []
    if early:
        first = levels // group - 1
        at = field_count - early
        block = second_ref[pl.ds(at, early), pl.ds(first * group, group)].reshape(early * group * width, owned)
        moved = picked(early_picks, block)
        for e in range(early):
            rows = moved[:, e * owned:(e + 1) * owned].reshape(devices, capacity, owned)
            early_ref[:, e * capacity:(e + 1) * capacity, :] = rows
        half = devices // 2
        sends.append(fetch(early_ref.at[pl.ds(half, half)], far_hbm, early_sem.at[0]))
        sends.append(fetch(early_ref.at[pl.ds(0, half)], near_hbm, early_sem.at[1]))
    group_rows = field_count * capacity
    aligned = group_rows % 8 == 0
    for number in range(levels // group):
        held = field_count - (early if number == levels // group - 1 else 0)
        blocks = second_ref[pl.ds(0, held), pl.ds(number * group, group)].reshape(held * group * width, owned)
        moved = picked(picks, blocks)
        for f in range(held):
            at = (number * field_count + f) * capacity
            send_ref[:, at:at + capacity, :] = moved[:, f * owned:(f + 1) * owned].reshape(devices, capacity, owned)
        if aligned:
            part = pl.ds(number * group_rows, held * capacity)
            sends.append(fetch(send_ref.at[:, part], send_hbm.at[:, part], send_sem.at[number]))
    if not aligned:
        sends.append(fetch(send_ref, send_hbm, send_sem.at[0]))

    tend_ref[...] = jnp.zeros_like(tend_ref)
    for f in range(field_count):
        for z in range(levels):
            gained = jnp.sum(second_ref[f, z] - crm_ref[f, z], axis=0, keepdims=True) * (1.0 / width)
            tend_ref[pl.ds(f * levels + z, 1), :] = gained
    small[3].wait()
    mass = mass_ref[...]
    fields = jnp.concatenate(
        [gcm_ref[f] for f in range(field_count)] + [mass, jnp.zeros((nodes, nodes - used - levels), jnp.float32)],
        axis=1,
    )
    factors = jnp.concatenate([mass] * field_count + [jnp.ones((nodes, nodes - used), jnp.float32)], axis=1)
    nodes_ref[...] = (fields + tend_ref[...].T) * factors
    return sends


def edges_y(elx, ely, side, nodes_ref, low_ref, high_ref):
    step = side * side
    for a in range(elx):
        first = a * ely * step
        final = (a * ely + ely - 1) * step + side - 1
        low_ref[a * side:(a + 1) * side, :] = nodes_ref[pl.ds(first, side, stride=side), :]
        high_ref[a * side:(a + 1) * side, :] = nodes_ref[pl.ds(final, side, stride=side), :]


def kernel_a(devices, capacity, early, elx, ely, side, *refs):
    sends = cloud_kernel(devices, capacity, early, *refs)
    edges_y(elx, ely, side, *refs[9:12])
    for copy in sends:
        copy.wait()


def divided(rows, levels, field, fields):
    mass = rows[:, fields * levels:(fields + 1) * levels]
    return rows[:, field * levels:(field + 1) * levels] / mass


def face_rows(elx, ely, side):
    step = side * side
    low = [b * step for b in range(ely)]
    return low, [((elx - 1) * ely + b) * step + (side - 1) * side for b in range(ely)]


def kernel_y(elx, ely, side, nodes_ref, south_ref, north_ref, part_ref, low_ref, high_ref, sum_ref, full_ref):
    step = side * side
    field_count, _, levels = part_ref.shape
    sum_ref[...] = nodes_ref[...]
    for a in range(elx):
        for b in range(ely):
            base = (a * ely + b) * step
            if b > 0:
                gain = nodes_ref[pl.ds(base - step + side - 1, side, stride=side), :]
            else:
                gain = south_ref[a * side:(a + 1) * side, :]
            here = pl.ds(base, side, stride=side)
            sum_ref[here, :] = nodes_ref[here, :] + gain
            if b + 1 < ely:
                gain = nodes_ref[pl.ds(base + step, side, stride=side), :]
            else:
                gain = north_ref[a * side:(a + 1) * side, :]
            here = pl.ds(base + side - 1, side, stride=side)
            sum_ref[here, :] = nodes_ref[here, :] + gain
    for face_ref, starts in zip((low_ref, high_ref), face_rows(elx, ely, side)):
        for b, start in enumerate(starts):
            face_ref[b * side:(b + 1) * side, :] = sum_ref[start:start + side, :]
    full_ref[...] = sum_ref[...]
    for a in range(elx - 1):
        for b in range(ely):
            last = (a * ely + b) * step + (side - 1) * side
            after = ((a + 1) * ely + b) * step
            joined = sum_ref[last:last + side, :] + sum_ref[after:after + side, :]
            full_ref[last:last + side, :] = joined
            full_ref[after:after + side, :] = joined
    full = full_ref[...]
    for f in range(field_count):
        part_ref[f] = divided(full, levels, f, field_count)


def complete_faces(elx, ely, side, low_ref, high_ref, west_ref, east_ref, gcm_ref):
    field_count, _, levels = gcm_ref.shape
    lows, highs = face_rows(elx, ely, side)
    for own_ref, sent_ref, starts in ((low_ref, west_ref, lows), (high_ref, east_ref, highs)):
        rows = own_ref[...] + sent_ref[...]
        for f in range(field_count):
            quotient = divided(rows, levels, f, field_count)
            for b, start in enumerate(starts):
                gcm_ref[f, start:start + side, :] = quotient[b * side:(b + 1) * side]


def turned_blocks(rows_of, out_hbm, out_ref, sem):
    block = out_ref.shape[0] // len(rows_of)
    copies = []
    for number, (step, slots_at) in enumerate(rows_of):
        here, there = pl.ds(number * block, block), pl.ds(step * block, block)
        out_ref[here, :] = slots_at().T
        copies.append(fetch(out_ref.at[here], out_hbm.at[there], sem.at[number]))
    return copies


def kernel_out(devices, capacity, groups, field_count, early, sizes, recv_ref, part_ref, west_ref, east_ref,
               low_ref, high_ref, *refs):
    out_hbm, gcm_hbm, out_ref, gcm_ref, spread_ref, sem, gcm_sem = refs[-7:]
    gcm_ref[...] = part_ref[...]
    complete_faces(*sizes, low_ref, high_ref, west_ref, east_ref, gcm_ref)
    gcm_copy = fetch(gcm_ref, gcm_hbm, gcm_sem)
    pitch = recv_ref.shape[0] // devices

    rows_ref = recv_ref
    if pitch % 16 == 0:
        rows_ref = spread_ref
        for source in range(devices):
            spread_ref[pl.ds(source * (pitch + 8), pitch), :] = recv_ref[pl.ds(source * pitch, pitch), :]
        pitch = pitch + 8

    def rows(first):
        ranked = [rows_ref[pl.ds(first + r, devices, stride=pitch), :] for r in range(capacity)]
        return jnp.concatenate(ranked, axis=0)

    blocks = groups * field_count - early
    steps = [(at % field_count) * groups + at // field_count for at in range(blocks)]
    rows_of = [(step, functools.partial(rows, at * capacity)) for at, step in enumerate(steps)]
    for copy in [gcm_copy] + turned_blocks(rows_of, out_hbm, out_ref, sem):
        copy.wait()


def kernel_early(devices, capacity, groups, field_count, early, sources, me_ref, *refs):
    apart = devices + 8
    slots = apart * capacity
    *blocks, out_hbm, row_ref, out_ref, sem = refs
    arrived = [(ref, index) for ref in blocks for index in range(ref.shape[0])]
    for (ref, index), bits in zip(arrived, sources):
        for e in range(early):
            tile = ref[index, pl.ds(e * capacity, capacity), :]
            row_ref[pl.ds(e * slots + (me_ref[0] ^ bits), capacity, stride=apart), :] = tile
    steps = [(field_count - early + e) * groups + groups - 1 for e in range(early)]

    def slots_at(first):
        ranked = [row_ref[first + r * apart:first + r * apart + devices, :] for r in range(capacity)]
        return jnp.concatenate(ranked, axis=0)

    rows_of = [(step, functools.partial(slots_at, e * slots)) for e, step in enumerate(steps)]
    for copy in turned_blocks(rows_of, out_hbm, out_ref, sem):
        copy.wait()


def params(mib):
    return pltpu.CompilerParams(vmem_limit_bytes=mib * MIB)


def cost(flops, byte_count):
    return pl.CostEstimate(flops=flops, bytes_accessed=byte_count, transcendentals=0)


def shift(face, axis, by):
    count = lax.axis_size(axis)
    return lax.ppermute(face, axis, [(i, (i + by) % count) for i in range(count)])


def exchange(block, bits):
    count = lax.axis_size(AXES)
    return lax.ppermute(block, AXES, [(i, i ^ bits) for i in range(count)])


def kernel_regroup(kept_ref, last_ref, *out_refs):
    count = kept_ref.shape[1] // len(out_refs)
    for number, out_ref in enumerate(out_refs):
        part = pl.ds(number * count, count)
        out_ref[0:1] = kept_ref[:, part]
        out_ref[1:2] = last_ref[:, part]


def regrouped(arrays, ways, first):
    count = arrays[0].shape[1] // ways
    if first:
        shape = jax.ShapeDtypeStruct((2, count) + arrays[0].shape[2:], arrays[0].dtype)
        return pl.pallas_call(
            kernel_regroup,
            out_shape=[shape] * ways,
            compiler_params=params(8),
            cost_estimate=cost(REGROUP_FLOPS, 10**6),
            name="regroup",
        )(*arrays)
    return [jnp.concatenate([a[:, i * count:(i + 1) * count] for a in arrays]) for i in range(ways)]


def hops(near, far, devices):
    top, *others = hop_bits(devices)
    arrays = [near[None], exchange(far, 1 << top)[None]]
    senders = [0, 1 << top]
    middle = len(others) - 1
    steps = [others[:1], others[1:middle], others[middle:]]
    for step in steps:
        moves = [0]
        for bit in step:
            moves = [move | flip for move in moves for flip in (0, 1 << bit)]
        parts = regrouped(arrays, len(moves), step is steps[0])
        arrays = [exchange(part, move) if move else part for part, move in zip(parts, moves)]
        senders = [sender ^ move for move in moves for sender in senders]
    return [array[:, 0] for array in arrays], senders


def body(crm_state, gcm_state, mass, dest, cost_class):
    devices = lax.axis_size(("ex", "ey"))
    field_count, levels, width, owned = crm_state.shape
    elx, ely, side = gcm_state.shape[2:5]
    capacity = max(2, 2 * owned // devices)
    slots = capacity * devices
    values = field_count * levels * width
    f32 = jnp.float32
    gcm_nodes = gcm_state.transpose(0, 2, 3, 4, 5, 1).reshape(field_count, owned, levels)
    mass_nodes = mass.transpose(1, 2, 3, 4, 0).reshape(owned, levels)
    sizes = (elx, ely, side)
    face_x = jax.ShapeDtypeStruct((ely * side, owned), f32)
    face_y = jax.ShapeDtypeStruct((elx * side, owned), f32)
    in_hbm = pl.BlockSpec(memory_space=pltpu.HBM)
    in_vmem = pl.BlockSpec(memory_space=pltpu.VMEM)
    square = jax.ShapeDtypeStruct((owned, owned), f32)
    in_smem = pl.BlockSpec(memory_space=pltpu.SMEM)
    me = lax.axis_index(AXES).astype(jnp.int32).reshape(1)
    groups = levels * width // owned
    early = EARLY_BLOCKS if capacity % 8 == 0 and devices & (devices - 1) == 0 else 0
    packed = (devices, (values // owned - early) * capacity, owned)
    apart = (max(2, devices) // 2, max(1, early) * capacity, owned)
    send, far, near, nodes, low, high = pl.pallas_call(
        functools.partial(kernel_a, devices, capacity, early, *sizes),
        out_shape=(
            jax.ShapeDtypeStruct(packed, f32),
            jax.ShapeDtypeStruct(apart, f32),
            jax.ShapeDtypeStruct(apart, f32),
            square,
            face_y,
            face_y,
        ),
        in_specs=[in_smem] + [in_hbm] * 5,
        out_specs=(in_hbm, in_hbm, in_hbm, in_vmem, in_vmem, in_vmem),
        scratch_shapes=[
            pltpu.VMEM(crm_state.shape, f32),
            pltpu.VMEM(crm_state.shape, f32),
            pltpu.VMEM((owned, owned), f32),
            pltpu.VMEM((owned, owned), f32),
            pltpu.VMEM(crm_state.shape, f32),
            pltpu.VMEM(gcm_nodes.shape, f32),
            pltpu.VMEM(mass_nodes.shape, f32),
            pltpu.VMEM((1, owned), jnp.int32),
            pltpu.VMEM((1, owned), jnp.int32),
            pltpu.VMEM(packed, f32),
            pltpu.VMEM((devices,) + apart[1:], f32),
            pltpu.SemaphoreType.DMA((4,)),
            pltpu.SemaphoreType.DMA((groups,)),
            pltpu.SemaphoreType.DMA((groups,)),
            pltpu.SemaphoreType.DMA((2,)),
        ],
        compiler_params=params(63),
        name="cloud_models",
    )(me, crm_state, gcm_nodes, mass_nodes, dest.reshape(1, owned), cost_class.reshape(1, owned))
    received = lax.all_to_all(send, AXES, split_axis=0, concat_axis=0, tiled=True)
    if early:
        arrived, sources = hops(near, far, devices)
    north = shift(low, "ey", -1)
    south = shift(high, "ey", 1)
    part, low, high = pl.pallas_call(
        functools.partial(kernel_y, *sizes),
        out_shape=(jax.ShapeDtypeStruct((field_count, owned, levels), f32), face_x, face_x),
        scratch_shapes=[pltpu.VMEM((owned, owned), f32)] * 2,
        compiler_params=params(8),
        cost_estimate=cost(10**5, 10**5),
        name="edge_sum_second",
    )(nodes, south, north)
    east = shift(low, "ex", -1)
    west = shift(high, "ex", 1)
    if early:
        part, arrived[-1] = lax.optimization_barrier((part, arrived[-1]))
    out_shape = jax.ShapeDtypeStruct((values, slots), f32)
    block_count = values // owned
    begun = []
    if early:
        begun.append(pl.pallas_call(
            functools.partial(kernel_early, devices, capacity, groups, field_count, early, sources),
            in_specs=[in_smem] + [in_vmem] * len(arrived),
            out_specs=in_hbm,
            out_shape=out_shape,
            scratch_shapes=[
                pltpu.VMEM((early * (devices + 8) * capacity, owned), f32),
                pltpu.VMEM((early * owned, slots), f32),
                pltpu.SemaphoreType.DMA((early,)),
            ],
            compiler_params=params(8),
            cost_estimate=cost(EARLY_FLOPS, 10**6),
            name="early_slots",
        )(me, *arrived))
    cloud, gcm_out = pl.pallas_call(
        functools.partial(kernel_out, devices, capacity, groups, field_count, early, sizes),
        in_specs=[in_vmem] * 6 + [in_hbm] * len(begun),
        out_specs=(in_hbm, in_hbm),
        out_shape=(out_shape, jax.ShapeDtypeStruct((field_count, owned, levels), f32)),
        input_output_aliases={6: 0} if begun else {},
        scratch_shapes=[
            pltpu.VMEM(((block_count - early) * owned, slots), f32),
            pltpu.VMEM((field_count, owned, levels), f32),
            pltpu.VMEM((devices * ((block_count - early) * capacity + 8), owned), f32),
            pltpu.SemaphoreType.DMA((block_count - early,)),
            pltpu.SemaphoreType.DMA,
        ],
        compiler_params=params(16),
        name="cloud_slots",
    )(received.reshape(-1, owned), part, west, east, low, high, *begun)
    gcm_out = gcm_out.reshape(field_count, elx, ely, side, side, levels).transpose(0, 5, 1, 2, 3, 4)
    return cloud.reshape(field_count, levels, width, slots), gcm_out


def solution(mesh):
    return jax.shard_map(
        body,
        mesh=mesh,
        in_specs=(
            P(None, None, None, ("ex", "ey")),
            P(None, None, "ex", "ey", None, None),
            P(None, "ex", "ey", None, None),
            P(("ex", "ey"), None),
            P(("ex", "ey")),
        ),
        out_specs=(P(None, None, None, ("ex", "ey")), P(None, None, "ex", "ey", None, None)),
        check_vma=False,
    )
```
